32 devices in a mesh: off: 2 (over core), win: 16 (over z, y, x).
Axes of the slice: x: 2, y: 2, z: 4, core: 2. Of those that a mesh axis runs over, the one named last changes fastest.
Arguments:
- kernels: float32 [2, 16, 16, 64, 128], P('off', 'win'), may hold values from -6 to 6
- blocks: int32 [2, 16, 16, 128], P('off', 'win'), may hold values from 0 to 2047
- counts: int32 [2, 16, 16], P('off', 'win'), may hold values from 1 to 128, as said below
- ray_of: int32 [2, 16, 16, 128], P('off', 'win'), may hold values from 0 to 511
- slopes: float32 [2, 16, 512], P('off', 'win'), may hold values from -6 to 6
Outputs:
- update: float32 [64, 32768], P(None, 'win')
- data_vector: float32 [2, 16, 512], P('off', 'win')
The draws below stay inside these ranges and needn't reach their ends.
Inputs may be any that keep to these rules, and one draw needn't show every extreme that they name: `counts`: some event windows, drawn from the seed (each with chance one in four), carry more segments each than the rest; one owner, drawn from the seed, receives 128 live slots from every window of every offset class.
All inputs are finite; a program needn't handle non-finite values.
Results may differ from the reference program's by a relative error of at most 0.0003.
Values sent between devices are 32-bit elements; how exact they have to be, the bound alone decides.
A program may use at most 64 MiB of HBM per device.

```python
import jax
import jax.numpy as jnp
from jax import lax

CELLS = 64
CAP = 128
BLK_DEV = 2048
RAYS = 512
ITERS = 3
NBLK = 32768
N_OFF = 2
N_WIN = 16


def draw_counts(key, part):
    keys = jax.random.split(jax.random.fold_in(key, 7), 4)
    shape = (N_OFF, N_WIN, N_WIN)
    heavy = jax.random.randint(keys[0], (N_OFF, N_WIN, 1), 0, 4) == 0
    upper = jax.random.randint(keys[1], shape, CAP // 2, CAP + 1)
    lower = jax.random.randint(keys[2], shape, 1, max(1, CAP // 4) + 1)
    loads = jnp.where(heavy, upper, lower)
    full_owner = jax.random.randint(keys[3], (), 0, N_WIN)
    owners = jnp.arange(N_WIN, dtype=jnp.int32)[None, None, :]
    return jnp.where(owners == full_owner, CAP, loads).astype(jnp.int32)


def with_ends(result, rng, least, largest):
    index_at = [jax.random.randint(jax.random.fold_in(rng, axis), (), 0, length) for axis, length in enumerate(result.shape)]
    widest = result.shape.index(max(result.shape))
    beside = index_at[:widest] + [(index_at[widest] + 1) % result.shape[widest]] + index_at[widest + 1:]
    return result.at[tuple(index_at)].set(least).at[tuple(beside)].set(largest)


def block_levels(rng, extent, shards, smallest, largest):
    gain, own = 1.0, jax.random.fold_in(rng, 6)
    for dim, parts in shards:
        draws = jnp.exp(jax.random.uniform(jax.random.fold_in(own, dim), (parts,), jnp.float32, smallest / len(shards), largest / len(shards)))
        gain = gain * jnp.repeat(draws, extent[dim] // parts).reshape([-1 if axis == dim else 1 for axis in range(len(extent))])
    return gain


def bell_draw(key, extent, width, most, cuts=(), held_as=jnp.bfloat16):
    result = jax.random.normal(key, extent, jnp.float32) * width
    if len(cuts) > 0:
        result = block_levels(key, extent, cuts, -0.22, 0.18) * result
    return jnp.clip(result, min=-most, max=most).astype(held_as)


def setup_inputs(seed: int = 0) -> dict:
    key_of = jax.random.split(jax.random.key(seed), 6)
    kernels = bell_draw(key_of[0], (N_OFF, N_WIN, N_WIN, CELLS, CAP), 1.0, 6.0, ((0, 2), (1, 16)), jnp.float32)
    blocks = with_ends(jax.random.randint(key_of[1], (N_OFF, N_WIN, N_WIN, CAP), 0, BLK_DEV), jax.random.fold_in(key_of[1], 1), 0, BLK_DEV - 1).astype(jnp.int32)
    counts = draw_counts(jax.random.fold_in(key_of[5], 71), 0)
    ray_of = with_ends(jax.random.randint(key_of[3], (N_OFF, N_WIN, N_WIN, CAP), 0, RAYS), jax.random.fold_in(key_of[3], 1), 0, RAYS - 1).astype(jnp.int32)
    slopes = bell_draw(key_of[4], (N_OFF, N_WIN, RAYS), 1.0, 6.0, ((0, 2), (1, 16)), jnp.float32)
    return {"kernels": kernels, "blocks": blocks, "counts": counts, "ray_of": ray_of, "slopes": slopes}


def masked_rows(kernel_src, count_src):
    slots = lax.broadcasted_iota(jnp.int32, kernel_src.shape, 2)
    return jnp.where(slots < count_src[:, None, None], kernel_src, jnp.zeros_like(kernel_src))

def global_ids(block_src):
    owners = lax.broadcasted_iota(jnp.int32, block_src.shape, 0)
    return (owners * BLK_DEV + block_src).astype(jnp.int32)

def reference(kernels, blocks, counts, ray_of, slopes):
    sources = N_OFF * N_WIN
    kern_all = kernels.reshape(sources, N_WIN, CELLS, CAP)
    block_all = blocks.reshape(sources, N_WIN, CAP)
    count_all = counts.reshape(sources, N_WIN)
    ray_all = ray_of.reshape(sources, N_WIN, CAP)

    def forward(model):

        def one_source(packed):
            kernel_src, block_src, count_src, ray_src = packed
            rows = masked_rows(kernel_src, count_src)
            fetched = jnp.moveaxis(model[:, global_ids(block_src)], 0, 1)
            values = lax.optimization_barrier(jnp.sum(rows * fetched, axis=1))
            return jax.ops.segment_sum(values.reshape(-1), ray_src.reshape(-1), num_segments=RAYS)
        data = lax.map(one_source, (kern_all, block_all, count_all, ray_all))
        return data.reshape(N_OFF, N_WIN, RAYS)

    def adjoint(data):
        data_src = data.reshape(sources, RAYS)

        def one_source(grad, packed):
            kernel_src, block_src, count_src, ray_src, datum = packed
            rows = masked_rows(kernel_src, count_src)
            weights = datum[ray_src]
            contrib = jnp.moveaxis(rows * weights[:, None, :], 1, 0).reshape(CELLS, -1)
            grad = grad.at[:, global_ids(block_src).reshape(-1)].add(contrib)
            return (grad, None)
        start = jnp.zeros((CELLS, NBLK), jnp.float32)
        grad, unused = lax.scan(one_source, start, (kern_all, block_all, count_all, ray_all, data_src))
        return grad
    beta = jnp.sqrt(jnp.sum(slopes * slopes))
    data_vector = slopes / beta
    model_vec = adjoint(data_vector)
    alpha = jnp.sqrt(jnp.sum(model_vec * model_vec))
    model_vec = model_vec / alpha
    search = model_vec
    phibar = beta
    rhobar = alpha
    update = jnp.zeros((CELLS, NBLK), jnp.float32)
    for step in range(ITERS):
        data_vector = forward(model_vec) - alpha * data_vector
        beta = jnp.sqrt(jnp.sum(data_vector * data_vector))
        data_vector = data_vector / beta
        model_vec = adjoint(data_vector) - beta * model_vec
        alpha = jnp.sqrt(jnp.sum(model_vec * model_vec))
        model_vec = model_vec / alpha
        rho = jnp.sqrt(rhobar * rhobar + beta * beta)
        cosine = rhobar / rho
        sine = beta / rho
        theta = sine * alpha
        rhobar = -cosine * alpha
        phi = cosine * phibar
        phibar = sine * phibar
        update = update + phi / rho * search
        search = model_vec - theta / rho * search
    return (update, data_vector)
```

```python
import functools

import jax
import jax.numpy as jnp
from jax import lax
from jax.experimental import pallas as pl
from jax.experimental.pallas import tpu as pltpu
from jax.sharding import PartitionSpec as P

BLK_DEV = 2048
ITERS = 3
LOW = 256
HIGH = BLK_DEV // LOW
GROUP = 4
LANES = 128

F32 = jnp.float32
BF16 = jnp.bfloat16
MESH = pl.DeviceIdType.MESH


def split2(x):
    top = x.astype(BF16)
    rest = (x - top.astype(F32)).astype(BF16)
    return top, rest


def rows_of(x):
    a = x.astype(BF16).astype(F32)
    b = (x - a).astype(BF16).astype(F32)
    c = x - a - b
    shape = (16, x.shape[1])
    i = lax.broadcasted_iota(jnp.int32, shape, 0)
    wide = lambda y: jnp.broadcast_to(y, shape)
    zero = jnp.zeros(shape, F32)
    return jnp.where(i == 0, wide(a), jnp.where(i == 1, wide(b), jnp.where(i == 2, wide(c), zero))).astype(BF16)


def fold(x):
    return sum(x[:, i : i + LANES] for i in range(0, x.shape[1], LANES))


def kernel(
    offs, wins, kern_ref, block_ref, count_ref, ray_ref, slope_ref,
    out_ref, data_ref,
    rays1h, low1h, held, first_send, first_recv, w_send, w_recv, f_send, f_recv, s_send, s_recv,
    acc, vec, raw, upd, srch,
    send_sem, recv_sem, kern_send, kern_recv, pair_send, pair_recv,
):
    total = offs * wins
    cells = kern_ref.shape[1]
    part = cells // offs
    slots = kern_ref.shape[2]
    rays = slope_ref.shape[1]
    groups = total // GROUP
    width = GROUP * slots
    my_off = lax.axis_index("off")
    my_win = lax.axis_index("win")
    me = my_win * offs + my_off

    def place(index):
        return (lax.rem(index, offs), index // offs)

    def to_of(k):
        return lax.rem(me + k, total)

    def from_of(k):
        return lax.rem(me + total - k, total)

    barrier = pltpu.get_barrier_semaphore()

    @pl.loop(1, total)
    def _(k):
        pl.semaphore_signal(barrier, inc=1, device_id=place(to_of(k)), device_id_type=MESH)

    ray_iota = lax.broadcasted_iota(jnp.int32, (rays, slots), 0)
    lane = lax.broadcasted_iota(jnp.int32, (1, slots), 1)
    for p in range(wins):
        ids = jnp.where(lane < count_ref[p], ray_ref[p : p + 1, :], -1)
        rays1h[:, p * slots : (p + 1) * slots] = jnp.where(ray_iota == ids, 1.0, 0.0).astype(BF16)

    def take(data):
        return jnp.sum(jnp.dot(rows_of(data), rays1h[...], preferred_element_type=F32), axis=0, keepdims=True)

    def gather_rays(values):
        got = lax.dot_general(rows_of(values), rays1h[...], (((1,), (1,)), ((), ())), preferred_element_type=F32)
        return jnp.sum(got, axis=0, keepdims=True)

    def total_of(partials):
        return jnp.sum(jnp.sum(partials, axis=0), axis=1, keepdims=True)

    data = slope_ref[...]
    weights = take(data)
    partial = fold(data * data)
    for p in range(wins):
        ids = block_ref[p : p + 1, :]
        high = ids // LOW
        first_send[p, :, 0:slots] = weights[:, p * slots : (p + 1) * slots]
        first_send[p, :, slots : 2 * slots] = partial
        first_send[p, :, 2 * slots : 3 * slots] = (ids - high * LOW).astype(F32)
        first_send[p, :, 3 * slots : 4 * slots] = high.astype(F32)
    first_recv[0] = first_send[my_win]
    held[0] = kern_ref[my_win, pl.ds(pl.multiple_of(my_off * part, 8), part), :]

    pl.semaphore_wait(barrier, total - 1)

    @pl.loop(1, total)
    def _(k):
        dest = to_of(k)
        pltpu.make_async_remote_copy(
            src_ref=first_send.at[dest // offs], dst_ref=first_recv.at[k],
            send_sem=send_sem.at[0], recv_sem=recv_sem.at[0],
            device_id=place(dest), device_id_type=MESH,
        ).start()

    @pl.loop(1, total)
    def _(k):
        dest = to_of(k)
        half = pl.ds(pl.multiple_of(lax.rem(dest, offs) * part, 8), part)
        pltpu.make_async_remote_copy(
            src_ref=kern_ref.at[dest // offs, half, :], dst_ref=held.at[k],
            send_sem=kern_send, recv_sem=kern_recv.at[k // GROUP],
            device_id=place(dest), device_id_type=MESH,
        ).start()

    def bytes_in(ref, sem):
        pltpu.make_async_copy(ref, ref, sem).wait()

    def cat(pieces):
        return jnp.concatenate(pieces, axis=1)

    def highs(g):
        return cat([first_recv[g * GROUP + i, :, 3 * slots : 4 * slots] for i in range(GROUP)])

    def kern_of(g):
        return cat([held[g * GROUP + i] for i in range(GROUP)])

    def scatter_group(g, weight_of, scale):
        row = cat([weight_of(g * GROUP + i) for i in range(GROUP)]) / scale
        top, rest = split2(kern_of(g) * row)
        both = jnp.concatenate([top, rest], axis=0)
        high = jnp.broadcast_to(highs(g), both.shape)
        left = jnp.concatenate(
            [both * jnp.where(high == h, 1.0, 0.0).astype(BF16) for h in range(HIGH)], axis=0
        )
        acc[...] += lax.dot_general(left, low1h[g], (((1,), (1,)), ((), ())), preferred_element_type=F32)

    def collect(h):
        at = h * 2 * part
        return acc[at : at + part, :] + acc[at + part : at + 2 * part, :]

    def forward(step):
        square = jnp.zeros((part, LOW), F32)
        lefts = []
        for h in range(HIGH):
            piece = raw[h]
            square += piece * piece
            lefts += list(split2(piece))
        left = jnp.concatenate(lefts, axis=0)
        norm = fold(jnp.sum(square, axis=0, keepdims=True))

        @pl.loop(0, groups)
        def _(g):
            got = jnp.dot(left, low1h[g], preferred_element_type=F32)
            high = jnp.broadcast_to(highs(g), (part, width))
            fetched = jnp.zeros((part, width), F32)
            for h in range(HIGH):
                at = h * 2 * part
                fetched += jnp.where(high == h, got[at : at + part] + got[at + part : at + 2 * part], 0.0)
            values = jnp.sum(fetched * kern_of(g), axis=0, keepdims=True)
            for i in range(GROUP):
                f_send[step, g * GROUP + i, :, 0:slots] = values[:, i * slots : (i + 1) * slots]
                f_send[step, g * GROUP + i, :, slots : 2 * slots] = norm

        @pl.loop(1, total)
        def _(k):
            pltpu.make_async_remote_copy(
                src_ref=f_send.at[step, k], dst_ref=f_recv.at[step, me],
                send_sem=send_sem.at[1 + 2 * step], recv_sem=recv_sem.at[1 + 2 * step],
                device_id=place(from_of(k)), device_id_type=MESH,
            ).start()

        f_recv[step, me] = f_send[step, 0]
        bytes_in(f_recv.at[step, pl.ds(1, total - 1)], recv_sem.at[1 + 2 * step])

    bytes_in(first_recv.at[pl.ds(1, total - 1)], recv_sem.at[0])
    beta = jnp.sqrt(total_of(first_recv[:, :, slots : 2 * slots]))
    low_iota = lax.broadcasted_iota(jnp.int32, (LOW, slots), 0).astype(F32)

    @pl.loop(0, groups)
    def _(g):
        for i in range(GROUP):
            low = first_recv[g * GROUP + i, :, 2 * slots : 3 * slots]
            low1h[g, :, i * slots : (i + 1) * slots] = jnp.where(low_iota == low, 1.0, 0.0).astype(BF16)

    acc[...] = jnp.zeros_like(acc)
    first_weight = lambda k: first_recv[k, :, 0:slots]
    bytes_in(held.at[pl.ds(1, GROUP - 1)], kern_recv.at[0])
    scatter_group(0, first_weight, beta)

    @pl.loop(1, groups)
    def _(g):
        bytes_in(held.at[pl.ds(g * GROUP, GROUP)], kern_recv.at[g])
        scatter_group(g, first_weight, beta)

    for h in range(HIGH):
        raw[h] = collect(h)
    data = data / beta

    phibar = beta
    rhobar = theta_rho = sine = cosine = None
    for step in range(ITERS):
        forward(step)
        alpha = jnp.sqrt(total_of(f_recv[step, :, :, slots : 2 * slots]))
        terms = cat([
            sum(f_recv[step, p * offs + o, :, 0:slots] for o in range(offs)) for p in range(wins)
        ])
        data = gather_rays(terms) / alpha - alpha * data
        partial = fold(data * data)
        last = step == ITERS - 1
        if not last:
            weights = take(data)
            for p in range(wins):
                w_send[step, p, :, 0:slots] = weights[:, p * slots : (p + 1) * slots]
                w_send[step, p, :, slots : 2 * slots] = partial
        else:
            s_send[...] = partial

        @pl.loop(1, total)
        def _(k):
            dest = to_of(k)
            pltpu.make_async_remote_copy(
                src_ref=s_send if last else w_send.at[step, dest // offs],
                dst_ref=s_recv.at[k] if last else w_recv.at[step, k],
                send_sem=send_sem.at[2 + 2 * step], recv_sem=recv_sem.at[2 + 2 * step],
                device_id=place(dest), device_id_type=MESH,
            ).start()

        if step == 0:
            rhobar = alpha
        else:
            theta_rho = sine * alpha / rho
            rhobar = -cosine * alpha
        for h in range(HIGH):
            fresh = raw[h] / alpha
            vec[h] = fresh
            srch[my_off, h] = fresh if step == 0 else fresh - theta_rho * srch[my_off, h]
        if last:
            for other in range(1, offs):
                for which, ref in enumerate((upd, srch)):
                    pltpu.make_async_remote_copy(
                        src_ref=ref.at[my_off], dst_ref=ref.at[my_off],
                        send_sem=pair_send.at[which, other], recv_sem=pair_recv.at[which, other],
                        device_id=(lax.rem(my_off + other, offs), my_win), device_id_type=MESH,
                    ).start()
            s_recv[0] = s_send[...]
            bytes_in(s_recv.at[pl.ds(1, total - 1)], recv_sem.at[2 + 2 * step])
            beta = jnp.sqrt(total_of(s_recv[...]))
        else:
            w_recv[step, 0] = w_send[step, my_win]
            bytes_in(w_recv.at[step, pl.ds(1, total - 1)], recv_sem.at[2 + 2 * step])
            beta = jnp.sqrt(total_of(w_recv[step, :, :, slots : 2 * slots]))

        data = data / beta
        rho = jnp.sqrt(rhobar * rhobar + beta * beta)
        cosine = rhobar / rho
        sine = beta / rho
        phi = cosine * phibar
        phibar = sine * phibar
        if last:
            data_ref[...] = data
            for other in range(1, offs):
                for which, ref in enumerate((upd, srch)):
                    bytes_in(ref.at[0], pair_recv.at[which, other])
            for o in range(offs):
                for h in range(HIGH):
                    out_ref[o * part : (o + 1) * part, h * LOW : (h + 1) * LOW] = (
                        upd[o, h] + phi / rho * srch[o, h]
                    )
        else:
            acc[...] = jnp.zeros_like(acc)

            @pl.loop(0, groups)
            def _(g):
                scatter_group(g, lambda k: w_recv[step, k, :, 0:slots], beta)

            for h in range(HIGH):
                raw[h] = collect(h) - beta * vec[h]
                moved = phi / rho * srch[my_off, h]
                upd[my_off, h] = moved if step == 0 else upd[my_off, h] + moved

    bytes_in(first_recv.at[pl.ds(1, total - 1)], send_sem.at[0])
    bytes_in(held.at[pl.ds(1, total - 1)], kern_send)
    for step in range(ITERS):
        bytes_in(f_recv.at[step, pl.ds(1, total - 1)], send_sem.at[1 + 2 * step])
        if step < ITERS - 1:
            bytes_in(w_recv.at[step, pl.ds(1, total - 1)], send_sem.at[2 + 2 * step])
        else:
            bytes_in(s_recv.at[pl.ds(1, total - 1)], send_sem.at[2 + 2 * step])
    for other in range(1, offs):
        for which, ref in enumerate((upd, srch)):
            bytes_in(ref.at[0], pair_send.at[which, other])


def body(kernels, blocks, counts, ray_of, slopes):
    offs, wins = lax.axis_size("off"), lax.axis_size("win")
    total = offs * wins
    cells, slots = kernels.shape[3:]
    rays = slopes.shape[2]
    part = cells // offs
    groups = total // GROUP
    vmem = pl.BlockSpec(memory_space=pltpu.VMEM)
    model = (HIGH, part, LOW)
    update, data = pl.pallas_call(
        functools.partial(kernel, offs, wins),
        out_shape=(
            jax.ShapeDtypeStruct((cells, BLK_DEV), F32),
            jax.ShapeDtypeStruct((1, rays), F32),
        ),
        in_specs=[vmem, vmem, pl.BlockSpec(memory_space=pltpu.SMEM), vmem, vmem],
        out_specs=(vmem, vmem),
        scratch_shapes=[
            pltpu.VMEM((rays, wins * slots), BF16),
            pltpu.VMEM((groups, LOW, GROUP * slots), BF16),
            pltpu.VMEM((total, part, slots), F32),
            pltpu.VMEM((wins, 1, 4 * slots), F32),
            pltpu.VMEM((total, 1, 4 * slots), F32),
            pltpu.VMEM((ITERS - 1, wins, 1, 2 * slots), F32),
            pltpu.VMEM((ITERS - 1, total, 1, 2 * slots), F32),
            pltpu.VMEM((ITERS, total, 1, 2 * slots), F32),
            pltpu.VMEM((ITERS, total, 1, 2 * slots), F32),
            pltpu.VMEM((1, slots), F32),
            pltpu.VMEM((total, 1, slots), F32),
            pltpu.VMEM((HIGH * 2 * part, LOW), F32),
            pltpu.VMEM(model, F32),
            pltpu.VMEM(model, F32),
            pltpu.VMEM((offs,) + model, F32),
            pltpu.VMEM((offs,) + model, F32),
            pltpu.SemaphoreType.DMA((2 * ITERS + 1,)),
            pltpu.SemaphoreType.DMA((2 * ITERS + 1,)),
            pltpu.SemaphoreType.DMA,
            pltpu.SemaphoreType.DMA((groups,)),
            pltpu.SemaphoreType.DMA((2, offs)),
            pltpu.SemaphoreType.DMA((2, offs)),
        ],
        compiler_params=pltpu.CompilerParams(
            collective_id=0, has_side_effects=True, vmem_limit_bytes=48 * 1024 * 1024
        ),
    )(kernels[0, 0], blocks[0, 0], counts[0, 0], ray_of[0, 0], slopes[0])
    return update, data[None]


def solution(mesh):
    in_specs = (
        P("off", "win", None, None, None),
        P("off", "win", None, None),
        P("off", "win", None),
        P("off", "win", None, None),
        P("off", "win", None),
    )
    out_specs = (P(None, "win"), P("off", "win", None))
    return jax.shard_map(body, mesh=mesh, in_specs=in_specs, out_specs=out_specs, check_vma=False)
```

```python
import functools

import jax
import jax.numpy as jnp
from jax import lax
from jax.experimental import pallas as pl
from jax.experimental.pallas import tpu as pltpu
from jax.sharding import PartitionSpec as P

BLK_DEV = 2048
ITERS = 3
LOW = 256
HIGH = BLK_DEV // LOW
GROUP = 8
LANES = 128

F32 = jnp.float32
BF16 = jnp.bfloat16
MESH = pl.DeviceIdType.MESH


def split2(x):
    top = x.astype(BF16)
    rest = (x - top.astype(F32)).astype(BF16)
    return top, rest


def rows_of(x):
    a = x.astype(BF16).astype(F32)
    b = (x - a).astype(BF16).astype(F32)
    c = x - a - b
    shape = (8, x.shape[1])
    i = lax.broadcasted_iota(jnp.int32, shape, 0)
    wide = lambda y: jnp.broadcast_to(y, shape)
    zero = jnp.zeros(shape, F32)
    return jnp.where(i == 0, wide(a), jnp.where(i == 1, wide(b), jnp.where(i == 2, wide(c), zero)))


def fold(x):
    return sum(x[:, i : i + LANES] for i in range(0, x.shape[1], LANES))


def kernel(
    offs, wins, kern_hbm, block_hbm, count_hbm, ray_hbm, slope_hbm,
    out_ref, data_ref,
    block_ref, count_ref, ray_ref, slope_ref,
    rays1h, ray_high, low1h, high1h, held,
    first_send, first_recv, w_send, w_recv, f_send, f_recv, s_send, s_recv,
    acc, vec, raw, upd, srch,
    send_sem, recv_sem, kern_send, kern_recv, pair_send, pair_recv, load_sem,
):
    total = offs * wins
    part = kern_hbm.shape[1] // offs
    slots = kern_hbm.shape[2]
    ray_low = rays1h.shape[0]
    ray_parts = slope_ref.shape[1] // ray_low
    groups = total // GROUP
    width = GROUP * slots
    step_wins = GROUP // offs
    my_off = lax.axis_index("off")
    my_win = lax.axis_index("win")
    me = my_win * offs + my_off
    half = lambda o: pl.ds(pl.multiple_of(o * part, 8), part)
    off_to = [lax.rem(my_off + d, offs) for d in range(offs)]
    off_from = [lax.rem(my_off + offs - d, offs) for d in range(offs)]
    win_to = lambda d: lax.rem(my_win + d, wins)
    win_from = lambda d: lax.rem(my_win + wins - d, wins)

    def group_pairs(g):
        return [(i, g * step_wins + i // offs, i % offs) for i in range(GROUP)]

    def each_group(act):
        act(0, True)

        @pl.loop(1, groups)
        def _(g):
            act(g, False)

    loads = [
        pltpu.make_async_copy(src, dst, load_sem.at[i])
        for i, (src, dst) in enumerate(
            ((count_hbm, count_ref), (ray_hbm, ray_ref), (slope_hbm, slope_ref), (block_hbm, block_ref))
        )
    ]
    loads.append(pltpu.make_async_copy(kern_hbm.at[my_win, half(my_off), :], held.at[0], load_sem.at[4]))
    for load in loads:
        load.start()

    barrier = pltpu.get_barrier_semaphore()

    def greet(g, first):
        for i, dw, do in group_pairs(g):
            if not (first and i == 0):
                pl.semaphore_signal(
                    barrier, inc=1, device_id=(off_to[do], win_to(dw)), device_id_type=MESH
                )

    each_group(greet)
    for load in loads:
        load.wait()

    ray_iota = lax.broadcasted_iota(jnp.int32, (ray_low, slots), 0)
    lane = lax.broadcasted_iota(jnp.int32, (1, slots), 1)
    for p in range(wins):
        ids = ray_ref[p : p + 1, :]
        high = ids // ray_low
        low = jnp.where(lane < count_ref[p], ids - high * ray_low, -1)
        rays1h[:, p * slots : (p + 1) * slots] = jnp.where(ray_iota == low, 1.0, 0.0).astype(BF16)
        ray_high[:, p * slots : (p + 1) * slots] = jnp.broadcast_to(high, (8, slots))

    def cat(pieces):
        return jnp.concatenate(pieces, axis=1)

    def take(data):
        left = jnp.concatenate(
            [rows_of(data[:, r * ray_low : (r + 1) * ray_low]) for r in range(ray_parts)], axis=0
        ).astype(BF16)
        got = jnp.dot(left, rays1h[...], preferred_element_type=F32)
        high = ray_high[...]
        picked = sum(jnp.where(high == r, got[8 * r : 8 * r + 8], 0.0) for r in range(ray_parts))
        return jnp.sum(picked, axis=0, keepdims=True)

    def gather_rays(values):
        rows = rows_of(values)
        high = ray_high[...]
        left = jnp.concatenate(
            [jnp.where(high == r, rows, 0.0) for r in range(ray_parts)], axis=0
        ).astype(BF16)
        got = lax.dot_general(left, rays1h[...], (((1,), (1,)), ((), ())), preferred_element_type=F32)
        return cat([jnp.sum(got[8 * r : 8 * r + 8], axis=0, keepdims=True) for r in range(ray_parts)])

    def total_of(partials):
        return jnp.sum(jnp.sum(partials, axis=0), axis=1, keepdims=True)

    data = slope_ref[...]
    weights = take(data)
    partial = fold(data * data)
    for p in range(wins):
        ids = block_ref[p : p + 1, :]
        high = ids // LOW
        first_send[p, :, 0:slots] = weights[:, p * slots : (p + 1) * slots]
        first_send[p, :, slots : 2 * slots] = partial
        first_send[p, :, 2 * slots : 3 * slots] = (ids - high * LOW).astype(F32)
        first_send[p, :, 3 * slots : 4 * slots] = high.astype(F32)
    first_recv[0] = first_send[my_win]

    pl.semaphore_wait(barrier, total - 1)

    def to_owners(source_of, target_of, index):
        def send(g, first):
            for i, dw, do in group_pairs(g):
                if not (first and i == 0):
                    win = win_to(dw)
                    pltpu.make_async_remote_copy(
                        src_ref=source_of(win), dst_ref=target_of(g * GROUP + i),
                        send_sem=send_sem.at[index], recv_sem=recv_sem.at[index],
                        device_id=(off_to[do], win), device_id_type=MESH,
                    ).start()

        each_group(send)

    to_owners(lambda win: first_send.at[win], lambda k: first_recv.at[k], 0)

    def send_rows(g, first):
        for i, dw, do in group_pairs(g):
            if not (first and i == 0):
                win = win_to(dw)
                pltpu.make_async_remote_copy(
                    src_ref=kern_hbm.at[win, half(off_to[do]), :], dst_ref=held.at[g * GROUP + i],
                    send_sem=kern_send, recv_sem=kern_recv.at[g],
                    device_id=(off_to[do], win), device_id_type=MESH,
                ).start()

    each_group(send_rows)

    def bytes_in(ref, sem):
        pltpu.make_async_copy(ref, ref, sem).wait()

    def kern_of(g):
        return cat([held[g * GROUP + i] for i in range(GROUP)])

    def scatter_group(g, weight_of, scale):
        row = cat([weight_of(g * GROUP + i) for i in range(GROUP)]) / scale
        parts = split2(kern_of(g) * row)
        rows = []
        for h in range(HIGH):
            mask = jnp.concatenate([high1h[g, h]] * (part // 16), axis=0)
            rows.append(cat([piece * mask for piece in parts]))
        left = jnp.concatenate(rows, axis=0)
        low = low1h[g]
        acc[...] += lax.dot_general(
            left, cat([low, low]), (((1,), (1,)), ((), ())), preferred_element_type=F32
        )

    def collect(h):
        return acc[h * part : (h + 1) * part, :]

    def forward(step):
        square = jnp.zeros((part, LOW), F32)
        lefts = []
        for h in range(HIGH):
            piece = raw[h]
            square += piece * piece
            lefts.append(cat(split2(piece)))
        left = jnp.concatenate(lefts, axis=0)
        norm = fold(jnp.sum(square, axis=0, keepdims=True))

        def terms_of(g, first):
            low = low1h[g]
            got = jnp.dot(left, jnp.concatenate([low, low], axis=0), preferred_element_type=F32)
            high = jnp.broadcast_to(
                cat([first_recv[g * GROUP + i, :, 3 * slots : 4 * slots] for i in range(GROUP)]), (8, width)
            )
            fetched = [jnp.zeros((8, width), F32)] * (part // 8)
            for h in range(HIGH):
                hit = high == h
                for r in range(part // 8):
                    at = h * part + r * 8
                    fetched[r] = jnp.where(hit, got[at : at + 8], fetched[r])
            rows = kern_of(g)
            mixed = sum(fetched[r] * rows[r * 8 : r * 8 + 8] for r in range(part // 8))
            values = jnp.sum(mixed, axis=0, keepdims=True)
            for i, dw, do in group_pairs(g):
                k = g * GROUP + i
                f_send[step, k, :, 0:slots] = values[:, i * slots : (i + 1) * slots]
                f_send[step, k, :, slots : 2 * slots] = norm
                if first and i == 0:
                    f_recv[step, me] = f_send[step, 0]
                else:
                    pltpu.make_async_remote_copy(
                        src_ref=f_send.at[step, k], dst_ref=f_recv.at[step, me],
                        send_sem=send_sem.at[1 + 2 * step], recv_sem=recv_sem.at[1 + 2 * step],
                        device_id=(off_from[do], win_from(dw)), device_id_type=MESH,
                    ).start()

        each_group(terms_of)
        bytes_in(f_recv.at[step, pl.ds(1, total - 1)], recv_sem.at[1 + 2 * step])

    bytes_in(first_recv.at[pl.ds(1, total - 1)], recv_sem.at[0])
    beta = jnp.sqrt(total_of(first_recv[:, :, slots : 2 * slots]))
    low_iota = lax.broadcasted_iota(jnp.int32, (LOW, slots), 0).astype(F32)

    @pl.loop(0, groups)
    def _(g):
        for i in range(GROUP):
            here = pl.ds(i * slots, slots)
            low = first_recv[g * GROUP + i, :, 2 * slots : 3 * slots]
            low1h[g, :, here] = jnp.where(low_iota == low, 1.0, 0.0).astype(BF16)
            high = jnp.broadcast_to(first_recv[g * GROUP + i, :, 3 * slots : 4 * slots], (16, slots))
            for h in range(HIGH):
                high1h[g, h, :, here] = jnp.where(high == h, 1.0, 0.0).astype(BF16)

    acc[...] = jnp.zeros_like(acc)

    def first_adjoint(g, first):
        begin = 1 if first else 0
        bytes_in(held.at[pl.ds(g * GROUP + begin, GROUP - begin)], kern_recv.at[g])
        scatter_group(g, lambda k: first_recv[k, :, 0:slots], beta)

    each_group(first_adjoint)

    for h in range(HIGH):
        raw[h] = collect(h)
    data = data / beta

    phibar = beta
    rho = rhobar = sine = cosine = None
    for step in range(ITERS):
        forward(step)
        alpha = jnp.sqrt(total_of(f_recv[step, :, :, slots : 2 * slots]))
        terms = cat([
            sum(f_recv[step, p * offs + o, :, 0:slots] for o in range(offs)) for p in range(wins)
        ])
        data = gather_rays(terms) / alpha - alpha * data
        partial = fold(data * data)
        last = step == ITERS - 1
        index = 2 + 2 * step
        if not last:
            weights = take(data)
            for p in range(wins):
                w_send[step, p, :, 0:slots] = weights[:, p * slots : (p + 1) * slots]
                w_send[step, p, :, slots : 2 * slots] = partial
            to_owners(lambda win: w_send.at[step, win], lambda k: w_recv.at[step, k], index)
        else:
            s_send[...] = partial
            to_owners(lambda win: s_send, lambda k: s_recv.at[k], index)

        if step == 0:
            rhobar = alpha
        else:
            theta_rho = sine * alpha / rho
            rhobar = -cosine * alpha
        for h in range(HIGH):
            fresh = raw[h] / alpha
            vec[h] = fresh
            srch[my_off, h] = fresh if step == 0 else fresh - theta_rho * srch[my_off, h]
        if last:
            for other in range(1, offs):
                for which, ref in enumerate((upd, srch)):
                    pltpu.make_async_remote_copy(
                        src_ref=ref.at[my_off], dst_ref=ref.at[my_off],
                        send_sem=pair_send.at[which, other], recv_sem=pair_recv.at[which, other],
                        device_id=(off_to[other], my_win), device_id_type=MESH,
                    ).start()
            s_recv[0] = s_send[...]
            bytes_in(s_recv.at[pl.ds(1, total - 1)], recv_sem.at[index])
            beta = jnp.sqrt(total_of(s_recv[...]))
        else:
            acc[...] = jnp.zeros_like(acc)
            w_recv[step, 0] = w_send[step, my_win]
            bytes_in(w_recv.at[step, pl.ds(1, total - 1)], recv_sem.at[index])
            beta = jnp.sqrt(total_of(w_recv[step, :, :, slots : 2 * slots]))

        data = data / beta
        rho = jnp.sqrt(rhobar * rhobar + beta * beta)
        cosine = rhobar / rho
        sine = beta / rho
        phi = cosine * phibar
        phibar = sine * phibar
        if last:
            data_ref[...] = data
            for other in range(1, offs):
                for which, ref in enumerate((upd, srch)):
                    bytes_in(ref.at[0], pair_recv.at[which, other])
            for o in range(offs):
                for h in range(HIGH):
                    out_ref[o * part : (o + 1) * part, h * LOW : (h + 1) * LOW] = (
                        upd[o, h] + phi / rho * srch[o, h]
                    )
        else:
            @pl.loop(0, groups)
            def _(g):
                scatter_group(g, lambda k: w_recv[step, k, :, 0:slots], beta)

            for h in range(HIGH):
                raw[h] = collect(h) - beta * vec[h]
                moved = phi / rho * srch[my_off, h]
                upd[my_off, h] = moved if step == 0 else upd[my_off, h] + moved

    bytes_in(first_recv.at[pl.ds(1, total - 1)], send_sem.at[0])
    bytes_in(held.at[pl.ds(1, total - 1)], kern_send)
    for step in range(ITERS):
        bytes_in(f_recv.at[step, pl.ds(1, total - 1)], send_sem.at[1 + 2 * step])
        if step < ITERS - 1:
            bytes_in(w_recv.at[step, pl.ds(1, total - 1)], send_sem.at[2 + 2 * step])
        else:
            bytes_in(s_recv.at[pl.ds(1, total - 1)], send_sem.at[2 + 2 * step])
    for other in range(1, offs):
        for which, ref in enumerate((upd, srch)):
            bytes_in(ref.at[0], pair_send.at[which, other])


def body(kernels, blocks, counts, ray_of, slopes):
    offs, wins = lax.axis_size("off"), lax.axis_size("win")
    total = offs * wins
    cells, slots = kernels.shape[3:]
    rays = slopes.shape[2]
    part = cells // offs
    groups = total // GROUP
    ray_low = LOW if rays % LOW == 0 else rays
    vmem = pl.BlockSpec(memory_space=pltpu.VMEM)
    model = (HIGH, part, LOW)
    update, data = pl.pallas_call(
        functools.partial(kernel, offs, wins),
        out_shape=(
            jax.ShapeDtypeStruct((cells, BLK_DEV), F32),
            jax.ShapeDtypeStruct((1, rays), F32),
        ),
        in_specs=[pl.BlockSpec(memory_space=pl.ANY)] * 5,
        out_specs=(vmem, vmem),
        scratch_shapes=[
            pltpu.VMEM((wins, slots), jnp.int32),
            pltpu.SMEM((wins,), jnp.int32),
            pltpu.VMEM((wins, slots), jnp.int32),
            pltpu.VMEM((1, rays), F32),
            pltpu.VMEM((ray_low, wins * slots), BF16),
            pltpu.VMEM((8, wins * slots), jnp.int32),
            pltpu.VMEM((groups, LOW, GROUP * slots), BF16),
            pltpu.VMEM((groups, HIGH, 16, GROUP * slots), BF16),
            pltpu.VMEM((total, part, slots), F32),
            pltpu.VMEM((wins, 1, 4 * slots), F32),
            pltpu.VMEM((total, 1, 4 * slots), F32),
            pltpu.VMEM((ITERS - 1, wins, 1, 2 * slots), F32),
            pltpu.VMEM((ITERS - 1, total, 1, 2 * slots), F32),
            pltpu.VMEM((ITERS, total, 1, 2 * slots), F32),
            pltpu.VMEM((ITERS, total, 1, 2 * slots), F32),
            pltpu.VMEM((1, slots), F32),
            pltpu.VMEM((total, 1, slots), F32),
            pltpu.VMEM((HIGH * part, LOW), F32),
            pltpu.VMEM(model, F32),
            pltpu.VMEM(model, F32),
            pltpu.VMEM((offs,) + model, F32),
            pltpu.VMEM((offs,) + model, F32),
            pltpu.SemaphoreType.DMA((2 * ITERS + 1,)),
            pltpu.SemaphoreType.DMA((2 * ITERS + 1,)),
            pltpu.SemaphoreType.DMA,
            pltpu.SemaphoreType.DMA((groups,)),
            pltpu.SemaphoreType.DMA((2, offs)),
            pltpu.SemaphoreType.DMA((2, offs)),
            pltpu.SemaphoreType.DMA((5,)),
        ],
        compiler_params=pltpu.CompilerParams(
            collective_id=0, has_side_effects=True, vmem_limit_bytes=48 * 1024 * 1024
        ),
    )(kernels[0, 0], blocks[0, 0], counts[0, 0], ray_of[0, 0], slopes[0])
    return update, data[None]


def solution(mesh):
    in_specs = (
        P("off", "win", None, None, None),
        P("off", "win", None, None),
        P("off", "win", None),
        P("off", "win", None, None),
        P("off", "win", None),
    )
    out_specs = (P(None, "win"), P("off", "win", None))
    return jax.shard_map(body, mesh=mesh, in_specs=in_specs, out_specs=out_specs, check_vma=False)
```

```python
import functools

import jax
import jax.numpy as jnp
from jax import lax
from jax.experimental import pallas as pl
from jax.experimental.pallas import tpu as pltpu
from jax.sharding import PartitionSpec as P

BLK_DEV = 2048
ITERS = 3
LOW = 256
HIGH = BLK_DEV // LOW
GROUP = 8
UNROLL = 4
LANES = 128

F32 = jnp.float32
BF16 = jnp.bfloat16
MESH = pl.DeviceIdType.MESH


def split2(x):
    top = x.astype(BF16)
    rest = (x - top.astype(F32)).astype(BF16)
    return top, rest


def rows_of(x):
    a = x.astype(BF16).astype(F32)
    b = (x - a).astype(BF16).astype(F32)
    c = x - a - b
    shape = (8, x.shape[1])
    i = lax.broadcasted_iota(jnp.int32, shape, 0)
    wide = lambda y: jnp.broadcast_to(y, shape)
    zero = jnp.zeros(shape, F32)
    return jnp.where(i == 0, wide(a), jnp.where(i == 1, wide(b), jnp.where(i == 2, wide(c), zero)))


def fold(x):
    return sum(x[:, i : i + LANES] for i in range(0, x.shape[1], LANES))


def kernel(
    offs, wins, kern_hbm, block_hbm, count_hbm, ray_hbm, slope_hbm,
    out_ref, data_ref,
    block_ref, count_ref, ray_ref, slope_ref,
    rays1h, ray_high, low1h, high1h, held,
    first_send, first_recv, w_send, w_recv, f_send, f_recv, s_send, s_recv,
    acc, vec, raw, upd, srch,
    send_sem, recv_sem, kern_send, kern_recv, pair_send, pair_recv, load_sem,
):
    kern_hbm, block_hbm, count_hbm, ray_hbm = (x.at[0, 0] for x in (kern_hbm, block_hbm, count_hbm, ray_hbm))
    slope_hbm = slope_hbm.at[0]
    total = offs * wins
    part = kern_hbm.shape[1] // offs
    slots = kern_hbm.shape[2]
    ray_low = rays1h.shape[0]
    ray_parts = slope_ref.shape[1] // ray_low
    groups = total // GROUP
    width = GROUP * slots
    step_wins = GROUP // offs
    my_off = lax.axis_index("off")
    my_win = lax.axis_index("win")
    me = my_win * offs + my_off
    half = lambda o: pl.ds(pl.multiple_of(o * part, 8), part)
    off_to = [lax.rem(my_off + d, offs) for d in range(offs)]
    off_from = [lax.rem(my_off + offs - d, offs) for d in range(offs)]
    win_to = lambda d: lax.rem(my_win + d, wins)
    win_from = lambda d: lax.rem(my_win + wins - d, wins)

    def group_pairs(g):
        return [(i, g * step_wins + i // offs, i % offs) for i in range(GROUP)]

    def each_group(act):
        middle = groups // 2
        if groups <= UNROLL:
            for j in range(groups):
                g = (middle + (2 * (j % 2) - 1) * ((j + 1) // 2)) % groups
                act(g, g == 0)
            return

        @pl.loop(0, groups - 1)
        def _(j):
            act(middle + (2 * lax.rem(j, 2) - 1) * ((j + 1) // 2), False)

        act(0, True)

    loads = [
        pltpu.make_async_copy(src, dst, load_sem.at[i])
        for i, (src, dst) in enumerate(
            ((count_hbm, count_ref), (ray_hbm, ray_ref), (slope_hbm, slope_ref), (block_hbm, block_ref))
        )
    ]
    loads.append(pltpu.make_async_copy(kern_hbm.at[my_win, half(my_off), :], held.at[0], load_sem.at[4]))
    for load in loads:
        load.start()

    barrier = pltpu.get_barrier_semaphore()

    def greet(g, first):
        for i, dw, do in group_pairs(g):
            if not (first and i == 0):
                pl.semaphore_signal(
                    barrier, inc=1, device_id=(off_to[do], win_to(dw)), device_id_type=MESH
                )

    each_group(greet)
    for load in loads:
        load.wait()

    ray_iota = lax.broadcasted_iota(jnp.int32, (ray_low, slots), 0)
    lane = lax.broadcasted_iota(jnp.int32, (1, slots), 1)
    for p in range(wins):
        ids = ray_ref[p : p + 1, :]
        high = ids // ray_low
        low = jnp.where(lane < count_ref[p], ids - high * ray_low, -1)
        rays1h[:, p * slots : (p + 1) * slots] = jnp.where(ray_iota == low, 1.0, 0.0).astype(BF16)
        ray_high[:, p * slots : (p + 1) * slots] = jnp.broadcast_to(high, (8, slots))

    def cat(pieces):
        return jnp.concatenate(pieces, axis=1)

    def take(data):
        left = jnp.concatenate(
            [rows_of(data[:, r * ray_low : (r + 1) * ray_low]) for r in range(ray_parts)], axis=0
        ).astype(BF16)
        got = jnp.dot(left, rays1h[...], preferred_element_type=F32)
        high = ray_high[...]
        picked = sum(jnp.where(high == r, got[8 * r : 8 * r + 8], 0.0) for r in range(ray_parts))
        return jnp.sum(picked, axis=0, keepdims=True)

    def gather_rays(values):
        rows = rows_of(values)
        high = ray_high[...]
        left = jnp.concatenate(
            [jnp.where(high == r, rows, 0.0) for r in range(ray_parts)], axis=0
        ).astype(BF16)
        got = lax.dot_general(left, rays1h[...], (((1,), (1,)), ((), ())), preferred_element_type=F32)
        return cat([jnp.sum(got[8 * r : 8 * r + 8], axis=0, keepdims=True) for r in range(ray_parts)])

    def total_of(partials):
        return jnp.sum(jnp.sum(partials, axis=0), axis=1, keepdims=True)

    data = slope_ref[...]
    weights = take(data)
    partial = fold(data * data)
    for p in range(wins):
        ids = block_ref[p : p + 1, :]
        high = ids // LOW
        first_send[p, :, 0:slots] = weights[:, p * slots : (p + 1) * slots]
        first_send[p, :, slots : 2 * slots] = partial
        first_send[p, :, 2 * slots : 3 * slots] = (ids - high * LOW).astype(F32)
        first_send[p, :, 3 * slots : 4 * slots] = high.astype(F32)
    first_recv[0] = first_send[my_win]

    pl.semaphore_wait(barrier, total - 1)

    def to_owners(source_of, target_of, index):
        def send(g, first):
            for i, dw, do in group_pairs(g):
                if not (first and i == 0):
                    win = win_to(dw)
                    pltpu.make_async_remote_copy(
                        src_ref=source_of(win), dst_ref=target_of(g * GROUP + i),
                        send_sem=send_sem.at[index], recv_sem=recv_sem.at[index],
                        device_id=(off_to[do], win), device_id_type=MESH,
                    ).start()

        each_group(send)

    to_owners(lambda win: first_send.at[win], lambda k: first_recv.at[k], 0)

    def send_rows(g, first):
        for i, dw, do in group_pairs(g):
            if not (first and i == 0):
                win = win_to(dw)
                pltpu.make_async_remote_copy(
                    src_ref=kern_hbm.at[win, half(off_to[do]), :], dst_ref=held.at[g * GROUP + i],
                    send_sem=kern_send, recv_sem=kern_recv.at[g],
                    device_id=(off_to[do], win), device_id_type=MESH,
                ).start()

    each_group(send_rows)

    def bytes_in(ref, sem):
        pltpu.make_async_copy(ref, ref, sem).wait()

    def kern_of(g):
        return cat([held[g * GROUP + i] for i in range(GROUP)])

    def scatter_group(g, weight_of, scale):
        row = cat([weight_of(g * GROUP + i) for i in range(GROUP)]) / scale
        parts = split2(kern_of(g) * row)
        rows = []
        for h in range(HIGH):
            mask = jnp.concatenate([high1h[g, h]] * (part // 16), axis=0)
            rows.append(cat([piece * mask for piece in parts]))
        left = jnp.concatenate(rows, axis=0)
        low = low1h[g]
        acc[...] += lax.dot_general(
            left, cat([low, low]), (((1,), (1,)), ((), ())), preferred_element_type=F32
        )

    def collect(h):
        return acc[h * part : (h + 1) * part, :]

    def forward(step):
        square = jnp.zeros((part, LOW), F32)
        lefts = []
        for h in range(HIGH):
            piece = raw[h]
            square += piece * piece
            lefts.append(cat(split2(piece)))
        left = jnp.concatenate(lefts, axis=0)
        norm = fold(jnp.sum(square, axis=0, keepdims=True))

        def terms_of(g, first):
            low = low1h[g]
            got = jnp.dot(left, jnp.concatenate([low, low], axis=0), preferred_element_type=F32)
            high = jnp.broadcast_to(
                cat([first_recv[g * GROUP + i, :, 3 * slots : 4 * slots] for i in range(GROUP)]), (8, width)
            )
            fetched = [jnp.zeros((8, width), F32)] * (part // 8)
            for h in range(HIGH):
                hit = high == h
                for r in range(part // 8):
                    at = h * part + r * 8
                    fetched[r] = jnp.where(hit, got[at : at + 8], fetched[r])
            rows = kern_of(g)
            mixed = sum(fetched[r] * rows[r * 8 : r * 8 + 8] for r in range(part // 8))
            values = jnp.sum(mixed, axis=0, keepdims=True)
            for i, dw, do in group_pairs(g):
                k = g * GROUP + i
                f_send[step, k, :, 0:slots] = values[:, i * slots : (i + 1) * slots]
                f_send[step, k, :, slots : 2 * slots] = norm
                if first and i == 0:
                    f_recv[step, me] = f_send[step, 0]
                else:
                    pltpu.make_async_remote_copy(
                        src_ref=f_send.at[step, k], dst_ref=f_recv.at[step, me],
                        send_sem=send_sem.at[1 + 2 * step], recv_sem=recv_sem.at[1 + 2 * step],
                        device_id=(off_from[do], win_from(dw)), device_id_type=MESH,
                    ).start()

        each_group(terms_of)
        bytes_in(f_recv.at[step, pl.ds(1, total - 1)], recv_sem.at[1 + 2 * step])

    bytes_in(first_recv.at[pl.ds(1, total - 1)], recv_sem.at[0])
    beta = jnp.sqrt(total_of(first_recv[:, :, slots : 2 * slots]))
    low_iota = lax.broadcasted_iota(jnp.int32, (LOW, slots), 0).astype(F32)

    @pl.loop(0, groups)
    def _(g):
        for i in range(GROUP):
            here = pl.ds(i * slots, slots)
            low = first_recv[g * GROUP + i, :, 2 * slots : 3 * slots]
            low1h[g, :, here] = jnp.where(low_iota == low, 1.0, 0.0).astype(BF16)
            high = jnp.broadcast_to(first_recv[g * GROUP + i, :, 3 * slots : 4 * slots], (16, slots))
            for h in range(HIGH):
                high1h[g, h, :, here] = jnp.where(high == h, 1.0, 0.0).astype(BF16)

    acc[...] = jnp.zeros_like(acc)

    def first_adjoint(g, first):
        begin = 1 if first else 0
        bytes_in(held.at[pl.ds(g * GROUP + begin, GROUP - begin)], kern_recv.at[g])
        scatter_group(g, lambda k: first_recv[k, :, 0:slots], beta)

    each_group(first_adjoint)

    for h in range(HIGH):
        raw[h] = collect(h)
    data = data / beta

    phibar = beta
    rho = rhobar = sine = cosine = None
    for step in range(ITERS):
        forward(step)
        alpha = jnp.sqrt(total_of(f_recv[step, :, :, slots : 2 * slots]))
        terms = cat([
            sum(f_recv[step, p * offs + o, :, 0:slots] for o in range(offs)) for p in range(wins)
        ])
        data = gather_rays(terms) / alpha - alpha * data
        partial = fold(data * data)
        last = step == ITERS - 1
        index = 2 + 2 * step
        if not last:
            weights = take(data)
            for p in range(wins):
                w_send[step, p, :, 0:slots] = weights[:, p * slots : (p + 1) * slots]
                w_send[step, p, :, slots : 2 * slots] = partial
            to_owners(lambda win: w_send.at[step, win], lambda k: w_recv.at[step, k], index)
        else:
            s_send[...] = partial
            to_owners(lambda win: s_send, lambda k: s_recv.at[k], index)

        if step == 0:
            rhobar = alpha
        else:
            theta_rho = sine * alpha / rho
            rhobar = -cosine * alpha
        for h in range(HIGH):
            fresh = raw[h] / alpha
            vec[h] = fresh
            srch[my_off, h] = fresh if step == 0 else fresh - theta_rho * srch[my_off, h]
        if last:
            for other in range(1, offs):
                for which, ref in enumerate((upd, srch)):
                    pltpu.make_async_remote_copy(
                        src_ref=ref.at[my_off], dst_ref=ref.at[my_off],
                        send_sem=pair_send.at[which, other], recv_sem=pair_recv.at[which, other],
                        device_id=(off_to[other], my_win), device_id_type=MESH,
                    ).start()
            s_recv[0] = s_send[...]
            bytes_in(s_recv.at[pl.ds(1, total - 1)], recv_sem.at[index])
            beta = jnp.sqrt(total_of(s_recv[...]))
        else:
            acc[...] = jnp.zeros_like(acc)
            w_recv[step, 0] = w_send[step, my_win]
            bytes_in(w_recv.at[step, pl.ds(1, total - 1)], recv_sem.at[index])
            beta = jnp.sqrt(total_of(w_recv[step, :, :, slots : 2 * slots]))

        data = data / beta
        rho = jnp.sqrt(rhobar * rhobar + beta * beta)
        cosine = rhobar / rho
        sine = beta / rho
        phi = cosine * phibar
        phibar = sine * phibar
        if last:
            data_ref[...] = data
            for other in range(1, offs):
                for which, ref in enumerate((upd, srch)):
                    bytes_in(ref.at[0], pair_recv.at[which, other])
            for o in range(offs):
                for h in range(HIGH):
                    out_ref[o * part : (o + 1) * part, h * LOW : (h + 1) * LOW] = (
                        upd[o, h] + phi / rho * srch[o, h]
                    )
        else:
            each_group(lambda g, first: scatter_group(g, lambda k: w_recv[step, k, :, 0:slots], beta))

            for h in range(HIGH):
                raw[h] = collect(h) - beta * vec[h]
                moved = phi / rho * srch[my_off, h]
                upd[my_off, h] = moved if step == 0 else upd[my_off, h] + moved

    bytes_in(first_recv.at[pl.ds(1, total - 1)], send_sem.at[0])
    bytes_in(held.at[pl.ds(1, total - 1)], kern_send)
    for step in range(ITERS):
        bytes_in(f_recv.at[step, pl.ds(1, total - 1)], send_sem.at[1 + 2 * step])
        if step < ITERS - 1:
            bytes_in(w_recv.at[step, pl.ds(1, total - 1)], send_sem.at[2 + 2 * step])
        else:
            bytes_in(s_recv.at[pl.ds(1, total - 1)], send_sem.at[2 + 2 * step])
    for other in range(1, offs):
        for which, ref in enumerate((upd, srch)):
            bytes_in(ref.at[0], pair_send.at[which, other])


def body(kernels, blocks, counts, ray_of, slopes):
    offs, wins = lax.axis_size("off"), lax.axis_size("win")
    total = offs * wins
    cells, slots = kernels.shape[3:]
    rays = slopes.shape[2]
    part = cells // offs
    groups = total // GROUP
    ray_low = LOW if rays % LOW == 0 else rays
    vmem = pl.BlockSpec(memory_space=pltpu.VMEM)
    model = (HIGH, part, LOW)
    update, data = pl.pallas_call(
        functools.partial(kernel, offs, wins),
        out_shape=(
            jax.ShapeDtypeStruct((cells, BLK_DEV), F32),
            jax.ShapeDtypeStruct((1, rays), F32),
        ),
        in_specs=[pl.BlockSpec(memory_space=pltpu.HBM)] * 5,
        out_specs=(vmem, vmem),
        scratch_shapes=[
            pltpu.VMEM((wins, slots), jnp.int32),
            pltpu.SMEM((wins,), jnp.int32),
            pltpu.VMEM((wins, slots), jnp.int32),
            pltpu.VMEM((1, rays), F32),
            pltpu.VMEM((ray_low, wins * slots), BF16),
            pltpu.VMEM((8, wins * slots), jnp.int32),
            pltpu.VMEM((groups, LOW, GROUP * slots), BF16),
            pltpu.VMEM((groups, HIGH, 16, GROUP * slots), BF16),
            pltpu.VMEM((total, part, slots), F32),
            pltpu.VMEM((wins, 1, 4 * slots), F32),
            pltpu.VMEM((total, 1, 4 * slots), F32),
            pltpu.VMEM((ITERS - 1, wins, 1, 2 * slots), F32),
            pltpu.VMEM((ITERS - 1, total, 1, 2 * slots), F32),
            pltpu.VMEM((ITERS, total, 1, 2 * slots), F32),
            pltpu.VMEM((ITERS, total, 1, 2 * slots), F32),
            pltpu.VMEM((1, slots), F32),
            pltpu.VMEM((total, 1, slots), F32),
            pltpu.VMEM((HIGH * part, LOW), F32),
            pltpu.VMEM(model, F32),
            pltpu.VMEM(model, F32),
            pltpu.VMEM((offs,) + model, F32),
            pltpu.VMEM((offs,) + model, F32),
            pltpu.SemaphoreType.DMA((2 * ITERS + 1,)),
            pltpu.SemaphoreType.DMA((2 * ITERS + 1,)),
            pltpu.SemaphoreType.DMA,
            pltpu.SemaphoreType.DMA((groups,)),
            pltpu.SemaphoreType.DMA((2, offs)),
            pltpu.SemaphoreType.DMA((2, offs)),
            pltpu.SemaphoreType.DMA((5,)),
        ],
        compiler_params=pltpu.CompilerParams(
            collective_id=0, has_side_effects=True, vmem_limit_bytes=60 * 1024 * 1024
        ),
    )(kernels, blocks, counts, ray_of, slopes)
    return update, data[None]


def solution(mesh):
    in_specs = (
        P("off", "win", None, None, None),
        P("off", "win", None, None),
        P("off", "win", None),
        P("off", "win", None, None),
        P("off", "win", None),
    )
    out_specs = (P(None, "win"), P("off", "win", None))
    return jax.shard_map(body, mesh=mesh, in_specs=in_specs, out_specs=out_specs, check_vma=False)
```

```python
import functools

import jax
import jax.numpy as jnp
from jax import lax
from jax.experimental import pallas as pl
from jax.experimental.pallas import tpu as pltpu
from jax.sharding import PartitionSpec as P

BLK_DEV = 2048
ITERS = 3
LOW = 256
HIGH = BLK_DEV // LOW
GROUP = 8
LANES = 128

F32 = jnp.float32
BF16 = jnp.bfloat16
MESH = pl.DeviceIdType.MESH


def split2(x):
    top = x.astype(BF16)
    rest = (x - top.astype(F32)).astype(BF16)
    return top, rest


def rows_of(x):
    a = x.astype(BF16).astype(F32)
    b = (x - a).astype(BF16).astype(F32)
    c = x - a - b
    shape = (8, x.shape[1])
    i = lax.broadcasted_iota(jnp.int32, shape, 0)
    wide = lambda y: jnp.broadcast_to(y, shape)
    zero = jnp.zeros(shape, F32)
    return jnp.where(i == 0, wide(a), jnp.where(i == 1, wide(b), jnp.where(i == 2, wide(c), zero)))


def fold(x):
    return sum(x[:, i : i + LANES] for i in range(0, x.shape[1], LANES))


def kernel(
    offs, wins, kern_hbm, block_hbm, count_hbm, ray_hbm, slope_hbm,
    out_ref, data_ref,
    block_ref, count_ref, ray_ref, slope_ref,
    rays1h, ray_high, low1h, high1h, held,
    ids_send, ids_recv, w_send, w_recv, f_send, f_recv, s_send, s_recv,
    acc, model, vec, raw, upd, srch,
    ids_sem, w_sem, f_sem, kern_send, kern_recv, pair_send, pair_recv, load_sem,
):
    kern_hbm, block_hbm, count_hbm, ray_hbm = (x.at[0, 0] for x in (kern_hbm, block_hbm, count_hbm, ray_hbm))
    slope_hbm = slope_hbm.at[0]
    total = offs * wins
    part = kern_hbm.shape[1] // offs
    slots = kern_hbm.shape[2]
    ray_low = rays1h.shape[0]
    ray_parts = slope_ref.shape[1] // ray_low
    groups = total // GROUP
    width = GROUP * slots
    step_wins = GROUP // offs
    my_off = lax.axis_index("off")
    my_win = lax.axis_index("win")
    me = my_win * offs + my_off
    half = lambda o: pl.ds(pl.multiple_of(o * part, 8), part)
    off_to = [lax.rem(my_off + d, offs) for d in range(offs)]
    off_from = [lax.rem(my_off + offs - d, offs) for d in range(offs)]
    win_to = lambda d: lax.rem(my_win + d, wins)
    win_from = lambda d: lax.rem(my_win + wins - d, wins)

    def group_at(j):
        return lax.rem(groups // 2 + (2 * lax.rem(j, 2) - 1) * ((j + 1) // 2) + groups, groups)

    def each_other(act):
        @pl.loop(0, groups)
        def _(j):
            g = group_at(j)

            @pl.loop(0, step_wins)
            def _(i):
                dw = g * step_wins + i
                for do in range(offs):
                    if do == 0:
                        pl.when(dw > 0)(lambda: act(g, dw * offs, dw, 0))
                    else:
                        act(g, dw * offs + do, dw, do)

    loads = [
        pltpu.make_async_copy(src, dst, load_sem.at[i])
        for i, (src, dst) in enumerate(
            ((count_hbm, count_ref), (ray_hbm, ray_ref), (slope_hbm, slope_ref), (block_hbm, block_ref))
        )
    ]
    loads.append(pltpu.make_async_copy(kern_hbm.at[my_win, half(my_off), :], held.at[0], load_sem.at[4]))
    for load in loads:
        load.start()

    barrier = pltpu.get_barrier_semaphore()
    each_other(lambda g, k, dw, do: pl.semaphore_signal(
        barrier, inc=1, device_id=(off_to[do], win_to(dw)), device_id_type=MESH
    ))
    for load in loads:
        load.wait()

    ray_iota = lax.broadcasted_iota(jnp.int32, (ray_low, slots), 0)
    lane = lax.broadcasted_iota(jnp.int32, (1, slots), 1)
    for p in range(wins):
        ids = ray_ref[p : p + 1, :]
        high = ids // ray_low
        low = jnp.where(lane < count_ref[p], ids - high * ray_low, -1)
        rays1h[:, p * slots : (p + 1) * slots] = jnp.where(ray_iota == low, 1.0, 0.0).astype(BF16)
        ray_high[:, p * slots : (p + 1) * slots] = jnp.broadcast_to(high, (8, slots))

    def cat(pieces):
        return jnp.concatenate(pieces, axis=1)

    def take(data):
        left = jnp.concatenate(
            [rows_of(data[:, r * ray_low : (r + 1) * ray_low]) for r in range(ray_parts)], axis=0
        ).astype(BF16)
        got = jnp.dot(left, rays1h[...], preferred_element_type=F32)
        high = ray_high[...]
        picked = sum(jnp.where(high == r, got[8 * r : 8 * r + 8], 0.0) for r in range(ray_parts))
        return jnp.sum(picked, axis=0, keepdims=True)

    def gather_rays(values):
        rows = rows_of(values)
        high = ray_high[...]
        left = jnp.concatenate(
            [jnp.where(high == r, rows, 0.0) for r in range(ray_parts)], axis=0
        ).astype(BF16)
        got = lax.dot_general(left, rays1h[...], (((1,), (1,)), ((), ())), preferred_element_type=F32)
        return cat([jnp.sum(got[8 * r : 8 * r + 8], axis=0, keepdims=True) for r in range(ray_parts)])

    def total_of(partials):
        return jnp.sum(jnp.sum(partials, axis=0), axis=1, keepdims=True)

    def bytes_in(ref, sem):
        pltpu.make_async_copy(ref, ref, sem).wait()

    for p in range(wins):
        ids = block_ref[p : p + 1, :]
        high = ids // LOW
        ids_send[p, :, 0:slots] = (ids - high * LOW).astype(F32)
        ids_send[p, :, slots : 2 * slots] = high.astype(F32)
    ids_recv[0] = ids_send[my_win]
    vec[...] = jnp.zeros_like(vec)
    srch[my_off] = jnp.zeros_like(vec)
    upd[my_off] = jnp.zeros_like(vec)
    raw[...] = jnp.zeros_like(raw)

    pl.semaphore_wait(barrier, total - 1)

    def to_owner(source_of, target_of, s_sem, r_sem_of):
        def send(g, k, dw, do):
            win = win_to(dw)
            pltpu.make_async_remote_copy(
                src_ref=source_of(win, do), dst_ref=target_of(k),
                send_sem=s_sem, recv_sem=r_sem_of(g),
                device_id=(off_to[do], win), device_id_type=MESH,
            ).start()

        each_other(send)

    to_owner(lambda win, do: ids_send.at[win], lambda k: ids_recv.at[k], ids_sem.at[0], lambda g: ids_sem.at[1])

    def kern_of(g):
        return cat([held[g * GROUP + i] for i in range(GROUP)])

    low_iota = lax.broadcasted_iota(jnp.int32, (LOW, slots), 0).astype(F32)

    def build_one_hots():
        bytes_in(ids_recv.at[pl.ds(1, total - 1)], ids_sem.at[1])

        @pl.loop(0, groups)
        def _(g):
            for i in range(GROUP):
                here = pl.ds(i * slots, slots)
                low = ids_recv[g * GROUP + i, :, 0:slots]
                low1h[g, :, here] = jnp.where(low_iota == low, 1.0, 0.0).astype(BF16)
                high = jnp.broadcast_to(ids_recv[g * GROUP + i, :, slots : 2 * slots], (16, slots))
                for h in range(HIGH):
                    high1h[g, h, :, here] = jnp.where(high == h, 1.0, 0.0).astype(BF16)

    def one_step(step, carry):
        data, alpha, rho, rhobar, phibar, sine, cosine = carry
        first = step == 0
        weights = take(data)
        partial = fold(data * data)
        for p in range(wins):
            w_send[step, p, :, 0:slots] = weights[:, p * slots : (p + 1) * slots]
            w_send[step, p, :, slots : 2 * slots] = partial
        to_owner(
            lambda win, do: w_send.at[step, win], lambda k: w_recv.at[step, k],
            w_sem.at[0, step], lambda g: w_sem.at[1, step],
        )

        @pl.when(first)
        def _():
            to_owner(
                lambda win, do: kern_hbm.at[win, half(off_to[do]), :], lambda k: held.at[k],
                kern_send, lambda g: kern_recv.at[g],
            )
            build_one_hots()

        theta_rho = sine * alpha / rho
        for h in range(HIGH):
            fresh = raw[h] / alpha
            vec[h] = fresh
            srch[my_off, h] = fresh - theta_rho * srch[my_off, h]
        acc[...] = jnp.zeros_like(acc)

        w_recv[step, 0] = w_send[step, my_win]
        bytes_in(w_recv.at[step, pl.ds(1, total - 1)], w_sem.at[1, step])
        beta = jnp.sqrt(total_of(w_recv[step, :, :, slots : 2 * slots]))
        data = data / beta
        rho = jnp.sqrt(rhobar * rhobar + beta * beta)
        cosine = rhobar / rho
        sine = beta / rho
        phi = cosine * phibar
        phibar = jnp.where(first, beta, sine * phibar)

        @pl.loop(0, groups)
        def _(j):
            g = group_at(j)

            @pl.when(first)
            def _():
                @pl.when(g > 0)
                def _():
                    bytes_in(held.at[pl.ds(g * GROUP, GROUP)], kern_recv.at[g])

                @pl.when(g == 0)
                def _():
                    bytes_in(held.at[pl.ds(1, GROUP - 1)], kern_recv.at[0])

            row = cat([w_recv[step, g * GROUP + i, :, 0:slots] for i in range(GROUP)]) / beta
            parts = split2(kern_of(g) * row)
            rows = []
            for h in range(HIGH):
                mask = jnp.concatenate([high1h[g, h]] * (part // 16), axis=0)
                rows.append(cat([piece * mask for piece in parts]))
            left = jnp.concatenate(rows, axis=0)
            low = low1h[g]
            acc[...] += lax.dot_general(
                left, cat([low, low]), (((1,), (1,)), ((), ())), preferred_element_type=F32
            )

        square = jnp.zeros((part, LOW), F32)
        for h in range(HIGH):
            piece = acc[h * part : (h + 1) * part, :] - beta * vec[h]
            raw[h] = piece
            square += piece * piece
            for c, half_piece in enumerate(split2(piece)):
                model[h * part : (h + 1) * part, c * LOW : (c + 1) * LOW] = half_piece
            upd[my_off, h] = upd[my_off, h] + phi / rho * srch[my_off, h]
        norm = fold(jnp.sum(square, axis=0, keepdims=True))

        @pl.loop(0, groups)
        def _(j):
            g = group_at(j)
            low = low1h[g]
            got = jnp.dot(model[...], jnp.concatenate([low, low], axis=0), preferred_element_type=F32)
            high = jnp.broadcast_to(
                cat([ids_recv[g * GROUP + i, :, slots : 2 * slots] for i in range(GROUP)]), (8, width)
            )
            fetched = [jnp.zeros((8, width), F32)] * (part // 8)
            for h in range(HIGH):
                hit = high == h
                for r in range(part // 8):
                    at = h * part + r * 8
                    fetched[r] = jnp.where(hit, got[at : at + 8], fetched[r])
            rows = kern_of(g)
            mixed = sum(fetched[r] * rows[r * 8 : r * 8 + 8] for r in range(part // 8))
            values = jnp.sum(mixed, axis=0, keepdims=True)
            for i in range(GROUP):
                k = g * GROUP + i
                f_send[step, k, :, 0:slots] = values[:, i * slots : (i + 1) * slots]
                f_send[step, k, :, slots : 2 * slots] = norm

            @pl.loop(0, step_wins)
            def _(i):
                dw = g * step_wins + i

                def send(do):
                    k = dw * offs + do
                    pltpu.make_async_remote_copy(
                        src_ref=f_send.at[step, k], dst_ref=f_recv.at[step, me],
                        send_sem=f_sem.at[0, step], recv_sem=f_sem.at[1, step],
                        device_id=(off_from[do], win_from(dw)), device_id_type=MESH,
                    ).start()

                pl.when(dw > 0)(lambda: send(0))
                for do in range(1, offs):
                    send(do)

        f_recv[step, me] = f_send[step, 0]
        bytes_in(f_recv.at[step, pl.ds(1, total - 1)], f_sem.at[1, step])
        alpha = jnp.sqrt(total_of(f_recv[step, :, :, slots : 2 * slots]))
        terms = cat([
            sum(f_recv[step, p * offs + o, :, 0:slots] for o in range(offs)) for p in range(wins)
        ])
        data = gather_rays(terms) / alpha - alpha * data
        rhobar = jnp.where(first, alpha, -cosine * alpha)
        sine = jnp.where(first, jnp.zeros_like(sine), sine)
        return data, alpha, rho, rhobar, phibar, sine, cosine

    one = jnp.ones((1, 1), F32)
    zero = jnp.zeros((1, 1), F32)
    data, alpha, rho, rhobar, phibar, sine, cosine = lax.fori_loop(
        0, ITERS, one_step, (slope_ref[...], one, one, zero, zero, zero, zero)
    )

    s_send[...] = fold(data * data)
    to_owner(lambda win, do: s_send, lambda k: s_recv.at[k], w_sem.at[0, ITERS], lambda g: w_sem.at[1, ITERS])
    theta_rho = sine * alpha / rho
    for h in range(HIGH):
        srch[my_off, h] = raw[h] / alpha - theta_rho * srch[my_off, h]
    for other in range(1, offs):
        for which, ref in enumerate((upd, srch)):
            pltpu.make_async_remote_copy(
                src_ref=ref.at[my_off], dst_ref=ref.at[my_off],
                send_sem=pair_send.at[which, other], recv_sem=pair_recv.at[which, other],
                device_id=(off_to[other], my_win), device_id_type=MESH,
            ).start()
    s_recv[0] = s_send[...]
    bytes_in(s_recv.at[pl.ds(1, total - 1)], w_sem.at[1, ITERS])
    beta = jnp.sqrt(total_of(s_recv[...]))
    data_ref[...] = data / beta
    rho = jnp.sqrt(rhobar * rhobar + beta * beta)
    phi = rhobar / rho * phibar
    for other in range(1, offs):
        for which, ref in enumerate((upd, srch)):
            bytes_in(ref.at[0], pair_recv.at[which, other])
    for o in range(offs):
        for h in range(HIGH):
            out_ref[o * part : (o + 1) * part, h * LOW : (h + 1) * LOW] = (
                upd[o, h] + phi / rho * srch[o, h]
            )

    bytes_in(ids_recv.at[pl.ds(1, total - 1)], ids_sem.at[0])
    bytes_in(held.at[pl.ds(1, total - 1)], kern_send)
    for step in range(ITERS):
        bytes_in(f_recv.at[step, pl.ds(1, total - 1)], f_sem.at[0, step])
        bytes_in(w_recv.at[step, pl.ds(1, total - 1)], w_sem.at[0, step])
    bytes_in(s_recv.at[pl.ds(1, total - 1)], w_sem.at[0, ITERS])
    for other in range(1, offs):
        for which, ref in enumerate((upd, srch)):
            bytes_in(ref.at[0], pair_send.at[which, other])


def body(kernels, blocks, counts, ray_of, slopes):
    offs, wins = lax.axis_size("off"), lax.axis_size("win")
    total = offs * wins
    cells, slots = kernels.shape[3:]
    rays = slopes.shape[2]
    part = cells // offs
    groups = total // GROUP
    ray_low = LOW if rays % LOW == 0 else rays
    vmem = pl.BlockSpec(memory_space=pltpu.VMEM)
    model = (HIGH, part, LOW)
    update, data = pl.pallas_call(
        functools.partial(kernel, offs, wins),
        out_shape=(
            jax.ShapeDtypeStruct((cells, BLK_DEV), F32),
            jax.ShapeDtypeStruct((1, rays), F32),
        ),
        in_specs=[pl.BlockSpec(memory_space=pltpu.HBM)] * 5,
        out_specs=(vmem, vmem),
        scratch_shapes=[
            pltpu.VMEM((wins, slots), jnp.int32),
            pltpu.SMEM((wins,), jnp.int32),
            pltpu.VMEM((wins, slots), jnp.int32),
            pltpu.VMEM((1, rays), F32),
            pltpu.VMEM((ray_low, wins * slots), BF16),
            pltpu.VMEM((8, wins * slots), jnp.int32),
            pltpu.VMEM((groups, LOW, GROUP * slots), BF16),
            pltpu.VMEM((groups, HIGH, 16, GROUP * slots), BF16),
            pltpu.VMEM((total, part, slots), F32),
            pltpu.VMEM((wins, 1, 2 * slots), F32),
            pltpu.VMEM((total, 1, 2 * slots), F32),
            pltpu.VMEM((ITERS, wins, 1, 2 * slots), F32),
            pltpu.VMEM((ITERS, total, 1, 2 * slots), F32),
            pltpu.VMEM((ITERS, total, 1, 2 * slots), F32),
            pltpu.VMEM((ITERS, total, 1, 2 * slots), F32),
            pltpu.VMEM((1, slots), F32),
            pltpu.VMEM((total, 1, slots), F32),
            pltpu.VMEM((HIGH * part, LOW), F32),
            pltpu.VMEM((HIGH * part, 2 * LOW), BF16),
            pltpu.VMEM(model, F32),
            pltpu.VMEM(model, F32),
            pltpu.VMEM((offs,) + model, F32),
            pltpu.VMEM((offs,) + model, F32),
            pltpu.SemaphoreType.DMA((2,)),
            pltpu.SemaphoreType.DMA((2, ITERS + 1)),
            pltpu.SemaphoreType.DMA((2, ITERS)),
            pltpu.SemaphoreType.DMA,
            pltpu.SemaphoreType.DMA((groups,)),
            pltpu.SemaphoreType.DMA((2, offs)),
            pltpu.SemaphoreType.DMA((2, offs)),
            pltpu.SemaphoreType.DMA((5,)),
        ],
        compiler_params=pltpu.CompilerParams(
            collective_id=0, has_side_effects=True, vmem_limit_bytes=60 * 1024 * 1024
        ),
    )(kernels, blocks, counts, ray_of, slopes)
    return update, data[None]


def solution(mesh):
    in_specs = (
        P("off", "win", None, None, None),
        P("off", "win", None, None),
        P("off", "win", None),
        P("off", "win", None, None),
        P("off", "win", None),
    )
    out_specs = (P(None, "win"), P("off", "win", None))
    return jax.shard_map(body, mesh=mesh, in_specs=in_specs, out_specs=out_specs, check_vma=False)
```

```python
import functools

import jax
import jax.numpy as jnp
from jax import lax
from jax.experimental import pallas as pl
from jax.experimental.pallas import tpu as pltpu
from jax.sharding import PartitionSpec as P

BLK_DEV = 2048
ITERS = 3
LOW = 256
HIGH = BLK_DEV // LOW
GROUP = 8
LANES = 128

F32 = jnp.float32
BF16 = jnp.bfloat16
MESH = pl.DeviceIdType.MESH


def split2(x):
    top = x.astype(BF16)
    rest = (x - top.astype(F32)).astype(BF16)
    return top, rest


def rows_of(x):
    a = x.astype(BF16).astype(F32)
    b = (x - a).astype(BF16).astype(F32)
    c = x - a - b
    shape = (8, x.shape[1])
    i = lax.broadcasted_iota(jnp.int32, shape, 0)
    wide = lambda y: jnp.broadcast_to(y, shape)
    zero = jnp.zeros(shape, F32)
    return jnp.where(i == 0, wide(a), jnp.where(i == 1, wide(b), jnp.where(i == 2, wide(c), zero)))


def fold(x):
    return sum(x[:, i : i + LANES] for i in range(0, x.shape[1], LANES))


def kernel(
    offs, wins, kern_hbm, block_hbm, count_hbm, ray_hbm, slope_hbm,
    out_ref, data_ref,
    block_ref, count_ref, ray_ref, slope_ref,
    rays1h, ray_high, low1h, high1h, arrived, held,
    ids_send, ids_recv, w_send, w_recv, f_send, f_swap, f_recv, s_send, s_recv, s_sum,
    acc, model, vec, raw, upd, srch,
    ids_sem, ids_pair, w_sem, w_pair, f_sem, f_pair, s_pair, kern_pair, kern_send, kern_recv, pair_send, pair_recv, load_sem,
):
    kern_hbm, block_hbm, count_hbm, ray_hbm = (x.at[0, 0] for x in (kern_hbm, block_hbm, count_hbm, ray_hbm))
    slope_hbm = slope_hbm.at[0]
    total = offs * wins
    part = kern_hbm.shape[1] // offs
    slots = kern_hbm.shape[2]
    ray_low = rays1h.shape[0]
    ray_parts = slope_ref.shape[1] // ray_low
    groups = total // GROUP
    width = GROUP * slots
    class_groups = wins // GROUP
    my_off = lax.axis_index("off")
    my_win = lax.axis_index("win")
    me = my_win * offs + my_off
    half = lambda o: pl.ds(pl.multiple_of(o * part, 8), part)
    off_to = [lax.rem(my_off + d, offs) for d in range(offs)]
    off_from = [lax.rem(my_off + offs - d, offs) for d in range(offs)]
    win_to = lambda d: lax.rem(my_win + d, wins)
    win_from = lambda d: lax.rem(my_win + wins - d, wins)

    def each_win(act):
        @pl.loop(1, wins)
        def _(d):
            act(d, win_to(d), win_from(d))

    def each_core(act):
        for c in range(1, offs):
            act(c, off_to[c], off_from[c])

    def remote(src, dst, s_sem, r_sem, core, win):
        pltpu.make_async_remote_copy(
            src_ref=src, dst_ref=dst, send_sem=s_sem, recv_sem=r_sem,
            device_id=(core, win), device_id_type=MESH,
        ).start()

    loads = [
        pltpu.make_async_copy(src, dst, load_sem.at[i])
        for i, (src, dst) in enumerate(
            ((count_hbm, count_ref), (ray_hbm, ray_ref), (slope_hbm, slope_ref), (block_hbm, block_ref))
        )
    ]
    loads.append(pltpu.make_async_copy(kern_hbm.at[my_win], arrived.at[0], load_sem.at[4]))
    for load in loads:
        load.start()

    barrier = pltpu.get_barrier_semaphore()
    greet = lambda core, win: pl.semaphore_signal(
        barrier, inc=1, device_id=(core, win), device_id_type=MESH
    )
    each_win(lambda d, to, _: greet(my_off, to))
    each_core(lambda c, to, _: greet(to, my_win))
    for load in loads:
        load.wait()

    ray_iota = lax.broadcasted_iota(jnp.int32, (ray_low, slots), 0)
    lane = lax.broadcasted_iota(jnp.int32, (1, slots), 1)
    for p in range(wins):
        ids = ray_ref[p : p + 1, :]
        high = ids // ray_low
        low = jnp.where(lane < count_ref[p], ids - high * ray_low, -1)
        rays1h[:, p * slots : (p + 1) * slots] = jnp.where(ray_iota == low, 1.0, 0.0).astype(BF16)
        ray_high[:, p * slots : (p + 1) * slots] = jnp.broadcast_to(high, (8, slots))

    def cat(pieces):
        return jnp.concatenate(pieces, axis=1)

    def take(data):
        left = jnp.concatenate(
            [rows_of(data[:, r * ray_low : (r + 1) * ray_low]) for r in range(ray_parts)], axis=0
        ).astype(BF16)
        got = jnp.dot(left, rays1h[...], preferred_element_type=F32)
        high = ray_high[...]
        picked = sum(jnp.where(high == r, got[8 * r : 8 * r + 8], 0.0) for r in range(ray_parts))
        return jnp.sum(picked, axis=0, keepdims=True)

    def gather_rays(values):
        rows = rows_of(values)
        high = ray_high[...]
        left = jnp.concatenate(
            [jnp.where(high == r, rows, 0.0) for r in range(ray_parts)], axis=0
        ).astype(BF16)
        got = lax.dot_general(left, rays1h[...], (((1,), (1,)), ((), ())), preferred_element_type=F32)
        return cat([jnp.sum(got[8 * r : 8 * r + 8], axis=0, keepdims=True) for r in range(ray_parts)])

    def total_of(partials):
        return jnp.sum(jnp.sum(partials, axis=0), axis=1, keepdims=True)

    def bytes_in(ref, sem):
        pltpu.make_async_copy(ref, ref, sem).wait()

    for p in range(wins):
        ids = block_ref[p : p + 1, :]
        high = ids // LOW
        ids_send[p, :, 0:slots] = (ids - high * LOW).astype(F32)
        ids_send[p, :, slots : 2 * slots] = high.astype(F32)
    ids_recv[0, 0] = ids_send[my_win]
    vec[...] = jnp.zeros_like(vec)
    srch[my_off] = jnp.zeros_like(vec)
    upd[my_off] = jnp.zeros_like(vec)
    raw[...] = jnp.zeros_like(raw)

    pl.semaphore_wait(barrier, wins - 1 + offs - 1)

    def to_owner(source_of, box, s_sem, r_sem):
        each_win(lambda d, to, _: remote(source_of(to), box.at[0, d], s_sem, r_sem, my_off, to))

    def swap(box, sems):
        each_core(lambda c, _, back: remote(box.at[0], box.at[c], sems.at[0, c], sems.at[1, c], back, my_win))

    def swapped(box, sems, side):
        for c in range(1, offs):
            bytes_in(box.at[c], sems.at[side, c])

    to_owner(lambda win: ids_send.at[win], ids_recv, ids_sem.at[0], ids_sem.at[1])

    def kern_of(k):
        return cat([held[k + i] for i in range(GROUP)])

    def pieces_of(box, k, begin):
        c, d = k // wins, lax.rem(k, wins)
        return cat([box[c, d + i, :, begin : begin + slots] for i in range(GROUP)])

    low_iota = lax.broadcasted_iota(jnp.int32, (LOW, width), 0).astype(F32)

    def build_one_hots():
        bytes_in(ids_recv.at[0, pl.ds(1, wins - 1)], ids_sem.at[1])
        swap(ids_recv, ids_pair)
        swapped(ids_recv, ids_pair, 1)

        @pl.loop(0, groups)
        def _(g):
            low = pieces_of(ids_recv, g * GROUP, 0)
            high = jnp.broadcast_to(pieces_of(ids_recv, g * GROUP, slots), (16, width))
            low1h[g] = jnp.where(low_iota == low, 1.0, 0.0).astype(BF16)
            for h in range(HIGH):
                high1h[g, h] = jnp.where(high == h, 1.0, 0.0).astype(BF16)

    def one_step(step, carry):
        data, alpha, rho, rhobar, phibar, sine, cosine = carry
        first = step == 0
        weights = take(data)
        partial = fold(data * data)
        for p in range(wins):
            w_send[step, p, :, 0:slots] = weights[:, p * slots : (p + 1) * slots]
            w_send[step, p, :, slots : 2 * slots] = partial
        to_owner(lambda win: w_send.at[step, win], w_recv.at[step], w_sem.at[0, step], w_sem.at[1, step])

        @pl.when(first)
        def _():
            each_win(lambda d, to, _: remote(
                kern_hbm.at[to], arrived.at[d], kern_send, kern_recv.at[d // GROUP], my_off, to
            ))
            build_one_hots()

        theta_rho = sine * alpha / rho
        for h in range(HIGH):
            fresh = raw[h] / alpha
            vec[h] = fresh
            srch[my_off, h] = fresh - theta_rho * srch[my_off, h]
        acc[...] = jnp.zeros_like(acc)

        w_recv[step, 0, 0] = w_send[step, my_win]
        bytes_in(w_recv.at[step, 0, pl.ds(1, wins - 1)], w_sem.at[1, step])
        swap(w_recv.at[step], w_pair.at[step])

        @pl.loop(0, groups)
        def _(g):
            k = g * GROUP

            @pl.when(first & (g < class_groups))
            def _():
                pl.when(g == 0)(lambda: bytes_in(arrived.at[pl.ds(1, GROUP - 1)], kern_recv.at[0]))
                pl.when(g > 0)(lambda: bytes_in(arrived.at[pl.ds(k, GROUP)], kern_recv.at[g]))
                for c in range(1, offs):
                    remote(
                        arrived.at[pl.ds(k, GROUP), half(off_from[c]), :],
                        held.at[pl.ds(c * wins + k, GROUP)],
                        kern_pair.at[0, c], kern_pair.at[1, c * class_groups + g], off_from[c], my_win,
                    )
                for i in range(GROUP):
                    held[k + i] = arrived[k + i, half(my_off), :]

            @pl.when(first & (g >= class_groups))
            def _():
                bytes_in(held.at[pl.ds(k, GROUP)], kern_pair.at[1, g])

            @pl.when(g == class_groups)
            def _():
                swapped(w_recv.at[step], w_pair.at[step], 1)

            row = pieces_of(w_recv.at[step], k, 0)
            parts = split2(kern_of(k) * row)
            rows = []
            for h in range(HIGH):
                mask = jnp.concatenate([high1h[g, h]] * (part // 16), axis=0)
                rows.append(cat([piece * mask for piece in parts]))
            left = jnp.concatenate(rows, axis=0)
            low = low1h[g]
            acc[...] += lax.dot_general(
                left, cat([low, low]), (((1,), (1,)), ((), ())), preferred_element_type=F32
            )

        norms = w_recv[step, :, :, :, slots : 2 * slots].reshape(total, 1, slots)
        beta = jnp.sqrt(total_of(norms))
        data = data / beta
        rho = jnp.sqrt(rhobar * rhobar + beta * beta)
        cosine = rhobar / rho
        sine = beta / rho
        phi = cosine * phibar
        phibar = jnp.where(first, beta, sine * phibar)

        square = jnp.zeros((part, LOW), F32)
        for h in range(HIGH):
            piece = acc[h * part : (h + 1) * part, :] / beta - beta * vec[h]
            raw[h] = piece
            square += piece * piece
            for c, half_piece in enumerate(split2(piece)):
                model[h * part : (h + 1) * part, c * LOW : (c + 1) * LOW] = half_piece
            upd[my_off, h] = upd[my_off, h] + phi / rho * srch[my_off, h]
        norm = fold(jnp.sum(square, axis=0, keepdims=True))

        @pl.loop(0, groups)
        def _(j):
            g = groups - 1 - j
            k = g * GROUP
            low = low1h[g]
            got = jnp.dot(model[...], jnp.concatenate([low, low], axis=0), preferred_element_type=F32)
            high = jnp.broadcast_to(pieces_of(ids_recv, k, slots), (8, width))
            fetched = [jnp.zeros((8, width), F32)] * (part // 8)
            for h in range(HIGH):
                hit = high == h
                for r in range(part // 8):
                    at = h * part + r * 8
                    fetched[r] = jnp.where(hit, got[at : at + 8], fetched[r])
            rows = kern_of(k)
            mixed = sum(fetched[r] * rows[r * 8 : r * 8 + 8] for r in range(part // 8))
            values = jnp.sum(mixed, axis=0, keepdims=True)
            c, d = k // wins, lax.rem(k, wins)
            for i in range(GROUP):
                f_send[step, c, d + i, :, 0:slots] = values[:, i * slots : (i + 1) * slots]
                f_send[step, c, d + i, :, slots : 2 * slots] = norm

            @pl.when(g == class_groups)
            def _():
                each_core(lambda c, to, _: remote(
                    f_send.at[step, c], f_swap.at[step, c], f_pair.at[0, step, c], f_pair.at[1, step, c],
                    to, my_win,
                ))

        for c in range(1, offs):
            bytes_in(f_swap.at[step, c], f_pair.at[1, step, c])
        f_send[step, 0] = f_send[step, 0] + sum(f_swap[step, c] for c in range(1, offs))
        each_win(lambda d, _, back: remote(
            f_send.at[step, 0, d], f_recv.at[step, my_win], f_sem.at[0, step], f_sem.at[1, step], my_off, back
        ))
        f_recv[step, my_win] = f_send[step, 0, 0]
        bytes_in(f_recv.at[step, pl.ds(1, wins - 1)], f_sem.at[1, step])
        alpha = jnp.sqrt(total_of(f_recv[step, :, :, slots : 2 * slots]))
        terms = cat([f_recv[step, p, :, 0:slots] for p in range(wins)])
        data = gather_rays(terms) / alpha - alpha * data
        rhobar = jnp.where(first, alpha, -cosine * alpha)
        sine = jnp.where(first, jnp.zeros_like(sine), sine)
        return data, alpha, rho, rhobar, phibar, sine, cosine

    one = jnp.ones((1, 1), F32)
    zero = jnp.zeros((1, 1), F32)
    data, alpha, rho, rhobar, phibar, sine, cosine = lax.fori_loop(
        0, ITERS, one_step, (slope_ref[...], one, one, zero, zero, zero, zero)
    )

    s_send[...] = fold(data * data)
    s_recv[0, 0] = s_send[...]
    to_owner(lambda win: s_send, s_recv, w_sem.at[0, ITERS], w_sem.at[1, ITERS])
    theta_rho = sine * alpha / rho
    for h in range(HIGH):
        srch[my_off, h] = raw[h] / alpha - theta_rho * srch[my_off, h]
    for other in range(1, offs):
        for which, ref in enumerate((upd, srch)):
            pltpu.make_async_remote_copy(
                src_ref=ref.at[my_off], dst_ref=ref.at[my_off],
                send_sem=pair_send.at[which, other], recv_sem=pair_recv.at[which, other],
                device_id=(off_to[other], my_win), device_id_type=MESH,
            ).start()
    bytes_in(s_recv.at[0, pl.ds(1, wins - 1)], w_sem.at[1, ITERS])
    s_sum[0] = jnp.sum(s_recv[0], axis=0)
    swap(s_sum, s_pair)
    swapped(s_sum, s_pair, 1)
    beta = jnp.sqrt(total_of(s_sum[...]))
    data_ref[...] = data / beta
    rho = jnp.sqrt(rhobar * rhobar + beta * beta)
    phi = rhobar / rho * phibar
    for other in range(1, offs):
        for which, ref in enumerate((upd, srch)):
            bytes_in(ref.at[0], pair_recv.at[which, other])
    for o in range(offs):
        for h in range(HIGH):
            out_ref[o * part : (o + 1) * part, h * LOW : (h + 1) * LOW] = (
                upd[o, h] + phi / rho * srch[o, h]
            )

    others = pl.ds(1, wins - 1)
    bytes_in(ids_recv.at[0, others], ids_sem.at[0])
    swapped(ids_recv, ids_pair, 0)
    bytes_in(arrived.at[others], kern_send)
    for c in range(1, offs):
        bytes_in(held.at[pl.ds(0, wins)], kern_pair.at[0, c])
    for step in range(ITERS):
        bytes_in(f_recv.at[step, others], f_sem.at[0, step])
        bytes_in(w_recv.at[step, 0, others], w_sem.at[0, step])
        swapped(w_recv.at[step], w_pair.at[step], 0)
        for c in range(1, offs):
            bytes_in(f_swap.at[step, c], f_pair.at[0, step, c])
    bytes_in(s_recv.at[0, others], w_sem.at[0, ITERS])
    swapped(s_sum, s_pair, 0)
    for other in range(1, offs):
        for which, ref in enumerate((upd, srch)):
            bytes_in(ref.at[0], pair_send.at[which, other])


def body(kernels, blocks, counts, ray_of, slopes):
    offs, wins = lax.axis_size("off"), lax.axis_size("win")
    total = offs * wins
    cells, slots = kernels.shape[3:]
    rays = slopes.shape[2]
    part = cells // offs
    groups = total // GROUP
    ray_low = LOW if rays % LOW == 0 else rays
    vmem = pl.BlockSpec(memory_space=pltpu.VMEM)
    model = (HIGH, part, LOW)
    update, data = pl.pallas_call(
        functools.partial(kernel, offs, wins),
        out_shape=(
            jax.ShapeDtypeStruct((cells, BLK_DEV), F32),
            jax.ShapeDtypeStruct((1, rays), F32),
        ),
        in_specs=[pl.BlockSpec(memory_space=pltpu.HBM)] * 5,
        out_specs=(vmem, vmem),
        scratch_shapes=[
            pltpu.VMEM((wins, slots), jnp.int32),
            pltpu.SMEM((wins,), jnp.int32),
            pltpu.VMEM((wins, slots), jnp.int32),
            pltpu.VMEM((1, rays), F32),
            pltpu.VMEM((ray_low, wins * slots), BF16),
            pltpu.VMEM((8, wins * slots), jnp.int32),
            pltpu.VMEM((groups, LOW, GROUP * slots), BF16),
            pltpu.VMEM((groups, HIGH, 16, GROUP * slots), BF16),
            pltpu.VMEM((wins, cells, slots), F32),
            pltpu.VMEM((total, part, slots), F32),
            pltpu.VMEM((wins, 1, 2 * slots), F32),
            pltpu.VMEM((offs, wins, 1, 2 * slots), F32),
            pltpu.VMEM((ITERS, wins, 1, 2 * slots), F32),
            pltpu.VMEM((ITERS, offs, wins, 1, 2 * slots), F32),
            pltpu.VMEM((ITERS, offs, wins, 1, 2 * slots), F32),
            pltpu.VMEM((ITERS, offs, wins, 1, 2 * slots), F32),
            pltpu.VMEM((ITERS, wins, 1, 2 * slots), F32),
            pltpu.VMEM((1, slots), F32),
            pltpu.VMEM((1, wins, 1, slots), F32),
            pltpu.VMEM((offs, 1, slots), F32),
            pltpu.VMEM((HIGH * part, LOW), F32),
            pltpu.VMEM((HIGH * part, 2 * LOW), BF16),
            pltpu.VMEM(model, F32),
            pltpu.VMEM(model, F32),
            pltpu.VMEM((offs,) + model, F32),
            pltpu.VMEM((offs,) + model, F32),
            pltpu.SemaphoreType.DMA((2,)),
            pltpu.SemaphoreType.DMA((2, offs)),
            pltpu.SemaphoreType.DMA((2, ITERS + 1)),
            pltpu.SemaphoreType.DMA((ITERS, 2, offs)),
            pltpu.SemaphoreType.DMA((2, ITERS)),
            pltpu.SemaphoreType.DMA((2, ITERS, offs)),
            pltpu.SemaphoreType.DMA((2, offs)),
            pltpu.SemaphoreType.DMA((2, groups)),
            pltpu.SemaphoreType.DMA,
            pltpu.SemaphoreType.DMA((groups,)),
            pltpu.SemaphoreType.DMA((2, offs)),
            pltpu.SemaphoreType.DMA((2, offs)),
            pltpu.SemaphoreType.DMA((5,)),
        ],
        compiler_params=pltpu.CompilerParams(
            collective_id=0, has_side_effects=True, vmem_limit_bytes=60 * 1024 * 1024
        ),
    )(kernels, blocks, counts, ray_of, slopes)
    return update, data[None]


def solution(mesh):
    in_specs = (
        P("off", "win", None, None, None),
        P("off", "win", None, None),
        P("off", "win", None),
        P("off", "win", None, None),
        P("off", "win", None),
    )
    out_specs = (P(None, "win"), P("off", "win", None))
    return jax.shard_map(body, mesh=mesh, in_specs=in_specs, out_specs=out_specs, check_vma=False)
```

```python
import functools

import jax
import jax.numpy as jnp
from jax import lax
from jax.experimental import pallas as pl
from jax.experimental.pallas import tpu as pltpu
from jax.sharding import PartitionSpec as P

BLK_DEV = 2048
ITERS = 3
LOW = 256
HIGH = BLK_DEV // LOW
GROUP = 8
LANES = 128

F32 = jnp.float32
BF16 = jnp.bfloat16
MESH = pl.DeviceIdType.MESH


def split2(x):
    top = x.astype(BF16)
    rest = (x - top.astype(F32)).astype(BF16)
    return top, rest


def rows_of(x):
    a = x.astype(BF16).astype(F32)
    b = (x - a).astype(BF16).astype(F32)
    c = x - a - b
    shape = (8, x.shape[1])
    i = lax.broadcasted_iota(jnp.int32, shape, 0)
    wide = lambda y: jnp.broadcast_to(y, shape)
    zero = jnp.zeros(shape, F32)
    return jnp.where(i == 0, wide(a), jnp.where(i == 1, wide(b), jnp.where(i == 2, wide(c), zero)))


def fold(x):
    return sum(x[:, i : i + LANES] for i in range(0, x.shape[1], LANES))


def kernel(
    offs, wins, kern_hbm, block_hbm, count_hbm, ray_hbm, slope_hbm,
    out_ref, data_ref,
    block_ref, count_ref, ray_ref, slope_ref,
    rays1h, rays1h_t, ray_high, low1h, low1h_t, high1h, arrived, held,
    ids_send, ids_recv, w_send, w_recv, f_send, f_swap, f_recv, s_send, s_recv, s_sum,
    acc, model, vec, raw, upd, srch,
    ids_sem, ids_pair, w_sem, w_pair, f_sem, f_pair, s_pair, kern_pair, kern_send, kern_recv, pair_send, pair_recv, load_sem,
):
    kern_hbm, block_hbm, count_hbm, ray_hbm = (x.at[0, 0] for x in (kern_hbm, block_hbm, count_hbm, ray_hbm))
    slope_hbm = slope_hbm.at[0]
    total = offs * wins
    part = kern_hbm.shape[1] // offs
    slots = kern_hbm.shape[2]
    ray_low = rays1h.shape[0]
    ray_parts = slope_ref.shape[1] // ray_low
    groups = total // GROUP
    width = GROUP * slots
    class_groups = wins // GROUP
    my_off = lax.axis_index("off")
    my_win = lax.axis_index("win")
    me = my_win * offs + my_off
    half = lambda o: pl.ds(pl.multiple_of(o * part, 8), part)
    off_to = [lax.rem(my_off + d, offs) for d in range(offs)]
    off_from = [lax.rem(my_off + offs - d, offs) for d in range(offs)]
    win_to = lambda d: lax.rem(my_win + d, wins)
    win_from = lambda d: lax.rem(my_win + wins - d, wins)

    def each_win(act):
        @pl.loop(1, wins)
        def _(d):
            act(d, win_to(d), win_from(d))

    def each_core(act):
        for c in range(1, offs):
            act(c, off_to[c], off_from[c])

    def remote(src, dst, s_sem, r_sem, core, win):
        pltpu.make_async_remote_copy(
            src_ref=src, dst_ref=dst, send_sem=s_sem, recv_sem=r_sem,
            device_id=(core, win), device_id_type=MESH,
        ).start()

    loads = [
        pltpu.make_async_copy(src, dst, load_sem.at[i])
        for i, (src, dst) in enumerate(
            ((count_hbm, count_ref), (ray_hbm, ray_ref), (slope_hbm, slope_ref), (block_hbm, block_ref))
        )
    ]
    loads.append(pltpu.make_async_copy(kern_hbm.at[my_win], arrived.at[0], load_sem.at[4]))
    for load in loads:
        load.start()

    barrier = pltpu.get_barrier_semaphore()
    greet = lambda core, win: pl.semaphore_signal(
        barrier, inc=1, device_id=(core, win), device_id_type=MESH
    )
    each_win(lambda d, to, _: greet(my_off, to))
    each_core(lambda c, to, _: greet(to, my_win))
    for load in loads:
        load.wait()

    ray_iota = lax.broadcasted_iota(jnp.int32, (ray_low, slots), 0)
    lane = lax.broadcasted_iota(jnp.int32, (1, slots), 1)
    for p in range(wins):
        ids = ray_ref[p : p + 1, :]
        high = ids // ray_low
        low = jnp.where(lane < count_ref[p], ids - high * ray_low, -1)
        rays1h[:, p * slots : (p + 1) * slots] = jnp.where(ray_iota == low, 1.0, 0.0).astype(BF16)
        ray_high[:, p * slots : (p + 1) * slots] = jnp.broadcast_to(high, (8, slots))

    def cat(pieces):
        return jnp.concatenate(pieces, axis=1)

    def take(data):
        left = jnp.concatenate(
            [rows_of(data[:, r * ray_low : (r + 1) * ray_low]) for r in range(ray_parts)], axis=0
        ).astype(BF16)
        got = jnp.dot(left, rays1h[...], preferred_element_type=F32)
        high = ray_high[...]
        picked = sum(jnp.where(high == r, got[8 * r : 8 * r + 8], 0.0) for r in range(ray_parts))
        return jnp.sum(picked, axis=0, keepdims=True)

    def gather_rays(values):
        rows = rows_of(values)
        high = ray_high[...]
        left = jnp.concatenate(
            [jnp.where(high == r, rows, 0.0) for r in range(ray_parts)], axis=0
        ).astype(BF16)
        got = jnp.dot(left, rays1h_t[...], preferred_element_type=F32)
        return cat([jnp.sum(got[8 * r : 8 * r + 8], axis=0, keepdims=True) for r in range(ray_parts)])

    def total_of(partials):
        return jnp.sum(jnp.sum(partials, axis=0), axis=1, keepdims=True)

    def bytes_in(ref, sem):
        pltpu.make_async_copy(ref, ref, sem).wait()

    for p in range(wins):
        ids = block_ref[p : p + 1, :]
        high = ids // LOW
        ids_send[p, :, 0:slots] = (ids - high * LOW).astype(F32)
        ids_send[p, :, slots : 2 * slots] = high.astype(F32)
    ids_recv[0, 0] = ids_send[my_win]
    vec[...] = jnp.zeros_like(vec)
    srch[my_off] = jnp.zeros_like(vec)
    upd[my_off] = jnp.zeros_like(vec)
    raw[...] = jnp.zeros_like(raw)

    pl.semaphore_wait(barrier, wins - 1 + offs - 1)

    def to_owner(source_of, box, s_sem, r_sem):
        each_win(lambda d, to, _: remote(source_of(to), box.at[0, d], s_sem, r_sem, my_off, to))

    def swap(box, sems):
        each_core(lambda c, _, back: remote(box.at[0], box.at[c], sems.at[0, c], sems.at[1, c], back, my_win))

    def swapped(box, sems, side):
        for c in range(1, offs):
            bytes_in(box.at[c], sems.at[side, c])

    to_owner(lambda win: ids_send.at[win], ids_recv, ids_sem.at[0], ids_sem.at[1])

    def kern_of(k):
        return cat([held[k + i] for i in range(GROUP)])

    def pieces_of(box, k, begin):
        c, d = k // wins, lax.rem(k, wins)
        return cat([box[c, d + i, :, begin : begin + slots] for i in range(GROUP)])

    low_iota = lax.broadcasted_iota(jnp.int32, (LOW, width), 0).astype(F32)

    def build_one_hots():
        @pl.loop(0, wins)
        def _(p):
            here = pl.ds(pl.multiple_of(p * slots, slots), slots)
            rays1h_t[here, :] = rays1h[:, here].astype(F32).T.astype(BF16)

        bytes_in(ids_recv.at[0, pl.ds(1, wins - 1)], ids_sem.at[1])
        swap(ids_recv, ids_pair)
        swapped(ids_recv, ids_pair, 1)

        @pl.loop(0, groups)
        def _(g):
            low = pieces_of(ids_recv, g * GROUP, 0)
            high = jnp.broadcast_to(pieces_of(ids_recv, g * GROUP, slots), (16, width))
            hot = jnp.where(low_iota == low, 1.0, 0.0)
            low1h[g] = hot.astype(BF16)
            low1h_t[g] = hot.T.astype(BF16)
            for h in range(HIGH):
                high1h[g, h] = jnp.where(high == h, 1.0, 0.0).astype(BF16)

    def one_step(step, carry):
        data, alpha, rho, rhobar, phibar, sine, cosine = carry
        first = step == 0
        weights = take(data)
        partial = fold(data * data)
        for p in range(wins):
            w_send[step, p, :, 0:slots] = weights[:, p * slots : (p + 1) * slots]
            w_send[step, p, :, slots : 2 * slots] = partial
        to_owner(lambda win: w_send.at[step, win], w_recv.at[step], w_sem.at[0, step], w_sem.at[1, step])

        @pl.when(first)
        def _():
            each_win(lambda d, to, _: remote(
                kern_hbm.at[to], arrived.at[d], kern_send, kern_recv.at[d // GROUP], my_off, to
            ))
            build_one_hots()

        theta_rho = sine * alpha / rho
        for h in range(HIGH):
            fresh = raw[h] / alpha
            vec[h] = fresh
            srch[my_off, h] = fresh - theta_rho * srch[my_off, h]
        acc[...] = jnp.zeros_like(acc)

        w_recv[step, 0, 0] = w_send[step, my_win]
        bytes_in(w_recv.at[step, 0, pl.ds(1, wins - 1)], w_sem.at[1, step])
        swap(w_recv.at[step], w_pair.at[step])

        @pl.loop(0, groups)
        def _(g):
            k = g * GROUP

            @pl.when(first & (g < class_groups))
            def _():
                pl.when(g == 0)(lambda: bytes_in(arrived.at[pl.ds(1, GROUP - 1)], kern_recv.at[0]))
                pl.when(g > 0)(lambda: bytes_in(arrived.at[pl.ds(k, GROUP)], kern_recv.at[g]))
                for c in range(1, offs):
                    remote(
                        arrived.at[pl.ds(k, GROUP), half(off_from[c]), :],
                        held.at[pl.ds(c * wins + k, GROUP)],
                        kern_pair.at[0, c], kern_pair.at[1, c * class_groups + g], off_from[c], my_win,
                    )
                for i in range(GROUP):
                    held[k + i] = arrived[k + i, half(my_off), :]

            @pl.when(first & (g >= class_groups))
            def _():
                bytes_in(held.at[pl.ds(k, GROUP)], kern_pair.at[1, g])

            @pl.when(g == class_groups)
            def _():
                swapped(w_recv.at[step], w_pair.at[step], 1)

            row = pieces_of(w_recv.at[step], k, 0)
            parts = split2(kern_of(k) * row)
            rows = []
            for h in range(HIGH):
                mask = jnp.concatenate([high1h[g, h]] * (part // 16), axis=0)
                rows.append(cat([piece * mask for piece in parts]))
            left = jnp.concatenate(rows, axis=0)
            low = low1h_t[g]
            acc[...] += jnp.dot(left, jnp.concatenate([low, low], axis=0), preferred_element_type=F32)

        norms = w_recv[step, :, :, :, slots : 2 * slots].reshape(total, 1, slots)
        beta = jnp.sqrt(total_of(norms))
        data = data / beta
        rho = jnp.sqrt(rhobar * rhobar + beta * beta)
        cosine = rhobar / rho
        sine = beta / rho
        phi = cosine * phibar
        phibar = jnp.where(first, beta, sine * phibar)

        square = jnp.zeros((part, LOW), F32)
        for h in range(HIGH):
            piece = acc[h * part : (h + 1) * part, :] / beta - beta * vec[h]
            raw[h] = piece
            square += piece * piece
            for c, half_piece in enumerate(split2(piece)):
                model[h * part : (h + 1) * part, c * LOW : (c + 1) * LOW] = half_piece
            upd[my_off, h] = upd[my_off, h] + phi / rho * srch[my_off, h]
        norm = fold(jnp.sum(square, axis=0, keepdims=True))

        @pl.loop(0, groups)
        def _(j):
            g = groups - 1 - j
            k = g * GROUP
            low = low1h[g]
            got = jnp.dot(model[...], jnp.concatenate([low, low], axis=0), preferred_element_type=F32)
            high = jnp.broadcast_to(pieces_of(ids_recv, k, slots), (8, width))
            fetched = [jnp.zeros((8, width), F32)] * (part // 8)
            for h in range(HIGH):
                hit = high == h
                for r in range(part // 8):
                    at = h * part + r * 8
                    fetched[r] = jnp.where(hit, got[at : at + 8], fetched[r])
            rows = kern_of(k)
            mixed = sum(fetched[r] * rows[r * 8 : r * 8 + 8] for r in range(part // 8))
            values = jnp.sum(mixed, axis=0, keepdims=True)
            c, d = k // wins, lax.rem(k, wins)
            for i in range(GROUP):
                f_send[step, c, d + i, :, 0:slots] = values[:, i * slots : (i + 1) * slots]
                f_send[step, c, d + i, :, slots : 2 * slots] = norm

            @pl.when(g == class_groups)
            def _():
                each_core(lambda c, to, _: remote(
                    f_send.at[step, c], f_swap.at[step, c], f_pair.at[0, step, c], f_pair.at[1, step, c],
                    to, my_win,
                ))

        for c in range(1, offs):
            bytes_in(f_swap.at[step, c], f_pair.at[1, step, c])
        f_send[step, 0] = f_send[step, 0] + sum(f_swap[step, c] for c in range(1, offs))
        each_win(lambda d, _, back: remote(
            f_send.at[step, 0, d], f_recv.at[step, my_win], f_sem.at[0, step], f_sem.at[1, step], my_off, back
        ))
        f_recv[step, my_win] = f_send[step, 0, 0]
        bytes_in(f_recv.at[step, pl.ds(1, wins - 1)], f_sem.at[1, step])
        alpha = jnp.sqrt(total_of(f_recv[step, :, :, slots : 2 * slots]))
        terms = cat([f_recv[step, p, :, 0:slots] for p in range(wins)])
        data = gather_rays(terms) / alpha - alpha * data
        rhobar = jnp.where(first, alpha, -cosine * alpha)
        sine = jnp.where(first, jnp.zeros_like(sine), sine)
        return data, alpha, rho, rhobar, phibar, sine, cosine

    one = jnp.ones((1, 1), F32)
    zero = jnp.zeros((1, 1), F32)
    data, alpha, rho, rhobar, phibar, sine, cosine = lax.fori_loop(
        0, ITERS, one_step, (slope_ref[...], one, one, zero, zero, zero, zero)
    )

    s_send[...] = fold(data * data)
    s_recv[0, 0] = s_send[...]
    to_owner(lambda win: s_send, s_recv, w_sem.at[0, ITERS], w_sem.at[1, ITERS])
    theta_rho = sine * alpha / rho
    for h in range(HIGH):
        srch[my_off, h] = raw[h] / alpha - theta_rho * srch[my_off, h]
    for other in range(1, offs):
        for which, ref in enumerate((upd, srch)):
            pltpu.make_async_remote_copy(
                src_ref=ref.at[my_off], dst_ref=ref.at[my_off],
                send_sem=pair_send.at[which, other], recv_sem=pair_recv.at[which, other],
                device_id=(off_to[other], my_win), device_id_type=MESH,
            ).start()
    bytes_in(s_recv.at[0, pl.ds(1, wins - 1)], w_sem.at[1, ITERS])
    s_sum[0] = jnp.sum(s_recv[0], axis=0)
    swap(s_sum, s_pair)
    swapped(s_sum, s_pair, 1)
    beta = jnp.sqrt(total_of(s_sum[...]))
    data_ref[...] = data / beta
    rho = jnp.sqrt(rhobar * rhobar + beta * beta)
    phi = rhobar / rho * phibar
    for other in range(1, offs):
        for which, ref in enumerate((upd, srch)):
            bytes_in(ref.at[0], pair_recv.at[which, other])
    for o in range(offs):
        for h in range(HIGH):
            out_ref[o * part : (o + 1) * part, h * LOW : (h + 1) * LOW] = (
                upd[o, h] + phi / rho * srch[o, h]
            )

    others = pl.ds(1, wins - 1)
    bytes_in(ids_recv.at[0, others], ids_sem.at[0])
    swapped(ids_recv, ids_pair, 0)
    bytes_in(arrived.at[others], kern_send)
    for c in range(1, offs):
        bytes_in(held.at[pl.ds(0, wins)], kern_pair.at[0, c])
    for step in range(ITERS):
        bytes_in(f_recv.at[step, others], f_sem.at[0, step])
        bytes_in(w_recv.at[step, 0, others], w_sem.at[0, step])
        swapped(w_recv.at[step], w_pair.at[step], 0)
        for c in range(1, offs):
            bytes_in(f_swap.at[step, c], f_pair.at[0, step, c])
    bytes_in(s_recv.at[0, others], w_sem.at[0, ITERS])
    swapped(s_sum, s_pair, 0)
    for other in range(1, offs):
        for which, ref in enumerate((upd, srch)):
            bytes_in(ref.at[0], pair_send.at[which, other])


def body(kernels, blocks, counts, ray_of, slopes):
    offs, wins = lax.axis_size("off"), lax.axis_size("win")
    total = offs * wins
    cells, slots = kernels.shape[3:]
    rays = slopes.shape[2]
    part = cells // offs
    groups = total // GROUP
    ray_low = LOW if rays % LOW == 0 else rays
    vmem = pl.BlockSpec(memory_space=pltpu.VMEM)
    model = (HIGH, part, LOW)
    update, data = pl.pallas_call(
        functools.partial(kernel, offs, wins),
        out_shape=(
            jax.ShapeDtypeStruct((cells, BLK_DEV), F32),
            jax.ShapeDtypeStruct((1, rays), F32),
        ),
        in_specs=[pl.BlockSpec(memory_space=pltpu.HBM)] * 5,
        out_specs=(vmem, vmem),
        scratch_shapes=[
            pltpu.VMEM((wins, slots), jnp.int32),
            pltpu.SMEM((wins,), jnp.int32),
            pltpu.VMEM((wins, slots), jnp.int32),
            pltpu.VMEM((1, rays), F32),
            pltpu.VMEM((ray_low, wins * slots), BF16),
            pltpu.VMEM((wins * slots, ray_low), BF16),
            pltpu.VMEM((8, wins * slots), jnp.int32),
            pltpu.VMEM((groups, LOW, GROUP * slots), BF16),
            pltpu.VMEM((groups, GROUP * slots, LOW), BF16),
            pltpu.VMEM((groups, HIGH, 16, GROUP * slots), BF16),
            pltpu.VMEM((wins, cells, slots), F32),
            pltpu.VMEM((total, part, slots), F32),
            pltpu.VMEM((wins, 1, 2 * slots), F32),
            pltpu.VMEM((offs, wins, 1, 2 * slots), F32),
            pltpu.VMEM((ITERS, wins, 1, 2 * slots), F32),
            pltpu.VMEM((ITERS, offs, wins, 1, 2 * slots), F32),
            pltpu.VMEM((ITERS, offs, wins, 1, 2 * slots), F32),
            pltpu.VMEM((ITERS, offs, wins, 1, 2 * slots), F32),
            pltpu.VMEM((ITERS, wins, 1, 2 * slots), F32),
            pltpu.VMEM((1, slots), F32),
            pltpu.VMEM((1, wins, 1, slots), F32),
            pltpu.VMEM((offs, 1, slots), F32),
            pltpu.VMEM((HIGH * part, LOW), F32),
            pltpu.VMEM((HIGH * part, 2 * LOW), BF16),
            pltpu.VMEM(model, F32),
            pltpu.VMEM(model, F32),
            pltpu.VMEM((offs,) + model, F32),
            pltpu.VMEM((offs,) + model, F32),
            pltpu.SemaphoreType.DMA((2,)),
            pltpu.SemaphoreType.DMA((2, offs)),
            pltpu.SemaphoreType.DMA((2, ITERS + 1)),
            pltpu.SemaphoreType.DMA((ITERS, 2, offs)),
            pltpu.SemaphoreType.DMA((2, ITERS)),
            pltpu.SemaphoreType.DMA((2, ITERS, offs)),
            pltpu.SemaphoreType.DMA((2, offs)),
            pltpu.SemaphoreType.DMA((2, groups)),
            pltpu.SemaphoreType.DMA,
            pltpu.SemaphoreType.DMA((groups,)),
            pltpu.SemaphoreType.DMA((2, offs)),
            pltpu.SemaphoreType.DMA((2, offs)),
            pltpu.SemaphoreType.DMA((5,)),
        ],
        compiler_params=pltpu.CompilerParams(
            collective_id=0, has_side_effects=True, vmem_limit_bytes=60 * 1024 * 1024
        ),
    )(kernels, blocks, counts, ray_of, slopes)
    return update, data[None]


def solution(mesh):
    in_specs = (
        P("off", "win", None, None, None),
        P("off", "win", None, None),
        P("off", "win", None),
        P("off", "win", None, None),
        P("off", "win", None),
    )
    out_specs = (P(None, "win"), P("off", "win", None))
    return jax.shard_map(body, mesh=mesh, in_specs=in_specs, out_specs=out_specs, check_vma=False)
```

```python
import functools

import jax
import jax.numpy as jnp
from jax import lax
from jax.experimental import pallas as pl
from jax.experimental.pallas import tpu as pltpu
from jax.sharding import PartitionSpec as P

BLK_DEV = 2048
ITERS = 3
LOW = 256
HIGH = BLK_DEV // LOW
GROUP = 8
LANES = 128

F32 = jnp.float32
BF16 = jnp.bfloat16
MESH = pl.DeviceIdType.MESH


def split2(x):
    top = x.astype(BF16)
    rest = (x - top.astype(F32)).astype(BF16)
    return top, rest


def rows_of(x):
    a = x.astype(BF16).astype(F32)
    b = (x - a).astype(BF16).astype(F32)
    c = x - a - b
    shape = (8, x.shape[1])
    i = lax.broadcasted_iota(jnp.int32, shape, 0)
    wide = lambda y: jnp.broadcast_to(y, shape)
    zero = jnp.zeros(shape, F32)
    return jnp.where(i == 0, wide(a), jnp.where(i == 1, wide(b), jnp.where(i == 2, wide(c), zero)))


def fold(x):
    return sum(x[:, i : i + LANES] for i in range(0, x.shape[1], LANES))


def kernel(
    offs, wins, kern_hbm, block_hbm, count_hbm, ray_hbm, slope_hbm,
    out_upd, out_srch, coef_ref, data_ref,
    block_ref, count_ref, ray_ref, slope_ref,
    rays1h, rays1h_t, ray_high, low1h, low1h_t, high1h, arrived, held,
    ids_send, ids_recv, w_send, w_recv, f_send, f_swap, f_recv, s_send, s_recv, s_sum,
    acc, model, vec, raw, upd, srch,
    ids_sem, ids_pair, w_sem, w_pair, f_sem, f_pair, s_pair, kern_pair, kern_send, kern_recv, pair_send, pair_recv, load_sem,
):
    kern_hbm, block_hbm, count_hbm, ray_hbm = (x.at[0, 0] for x in (kern_hbm, block_hbm, count_hbm, ray_hbm))
    slope_hbm = slope_hbm.at[0]
    total = offs * wins
    part = kern_hbm.shape[1] // offs
    slots = kern_hbm.shape[2]
    ray_low = rays1h.shape[0]
    ray_parts = slope_ref.shape[1] // ray_low
    groups = total // GROUP
    width = GROUP * slots
    class_groups = wins // GROUP
    my_off = lax.axis_index("off")
    my_win = lax.axis_index("win")
    me = my_win * offs + my_off
    half = lambda o: pl.ds(pl.multiple_of(o * part, 8), part)
    off_to = [lax.rem(my_off + d, offs) for d in range(offs)]
    off_from = [lax.rem(my_off + offs - d, offs) for d in range(offs)]
    win_to = lambda d: lax.rem(my_win + d, wins)
    win_from = lambda d: lax.rem(my_win + wins - d, wins)

    def each_win(act):
        @pl.loop(1, wins)
        def _(d):
            act(d, win_to(d), win_from(d))

    def each_core(act):
        for c in range(1, offs):
            act(c, off_to[c], off_from[c])

    def remote(src, dst, s_sem, r_sem, core, win):
        pltpu.make_async_remote_copy(
            src_ref=src, dst_ref=dst, send_sem=s_sem, recv_sem=r_sem,
            device_id=(core, win), device_id_type=MESH,
        ).start()

    loads = [
        pltpu.make_async_copy(src, dst, load_sem.at[i])
        for i, (src, dst) in enumerate(
            ((count_hbm, count_ref), (ray_hbm, ray_ref), (slope_hbm, slope_ref), (block_hbm, block_ref))
        )
    ]
    loads.append(pltpu.make_async_copy(kern_hbm.at[my_win], arrived.at[0], load_sem.at[4]))
    for load in loads:
        load.start()

    barrier = pltpu.get_barrier_semaphore()
    greet = lambda core, win: pl.semaphore_signal(
        barrier, inc=1, device_id=(core, win), device_id_type=MESH
    )
    each_win(lambda d, to, _: greet(my_off, to))
    each_core(lambda c, to, _: greet(to, my_win))
    for load in loads:
        load.wait()

    ray_iota = lax.broadcasted_iota(jnp.int32, (ray_low, slots), 0)
    lane = lax.broadcasted_iota(jnp.int32, (1, slots), 1)
    for p in range(wins):
        ids = ray_ref[p : p + 1, :]
        high = ids // ray_low
        low = jnp.where(lane < count_ref[p], ids - high * ray_low, -1)
        rays1h[:, p * slots : (p + 1) * slots] = jnp.where(ray_iota == low, 1.0, 0.0).astype(BF16)
        ray_high[:, p * slots : (p + 1) * slots] = jnp.broadcast_to(high, (8, slots))

    def cat(pieces):
        return jnp.concatenate(pieces, axis=1)

    def take(data):
        left = jnp.concatenate(
            [rows_of(data[:, r * ray_low : (r + 1) * ray_low]) for r in range(ray_parts)], axis=0
        ).astype(BF16)
        got = jnp.dot(left, rays1h[...], preferred_element_type=F32)
        high = ray_high[...]
        picked = sum(jnp.where(high == r, got[8 * r : 8 * r + 8], 0.0) for r in range(ray_parts))
        return jnp.sum(picked, axis=0, keepdims=True)

    def gather_rays(values):
        rows = rows_of(values)
        high = ray_high[...]
        left = jnp.concatenate(
            [jnp.where(high == r, rows, 0.0) for r in range(ray_parts)], axis=0
        ).astype(BF16)
        got = jnp.dot(left, rays1h_t[...], preferred_element_type=F32)
        return cat([jnp.sum(got[8 * r : 8 * r + 8], axis=0, keepdims=True) for r in range(ray_parts)])

    def total_of(partials):
        return jnp.sum(jnp.sum(partials, axis=0), axis=1, keepdims=True)

    def write_weights(step, data):
        weights = take(data)
        partial = fold(data * data)
        for p in range(wins):
            w_send[step, p, :, 0:slots] = weights[:, p * slots : (p + 1) * slots]
            w_send[step, p, :, slots : 2 * slots] = partial

    write_weights(0, slope_ref[...])

    def bytes_in(ref, sem):
        pltpu.make_async_copy(ref, ref, sem).wait()

    for p in range(wins):
        ids = block_ref[p : p + 1, :]
        high = ids // LOW
        ids_send[p, :, 0:slots] = (ids - high * LOW).astype(F32)
        ids_send[p, :, slots : 2 * slots] = high.astype(F32)
    ids_recv[0, 0] = ids_send[my_win]
    vec[...] = jnp.zeros_like(vec)
    srch[...] = jnp.zeros_like(vec)
    upd[...] = jnp.zeros_like(vec)
    raw[...] = jnp.zeros_like(raw)

    pl.semaphore_wait(barrier, wins - 1 + offs - 1)

    def to_owner(source_of, box, s_sem, r_sem):
        each_win(lambda d, to, _: remote(source_of(to), box.at[0, d], s_sem, r_sem, my_off, to))

    def swap(box, sems):
        each_core(lambda c, _, back: remote(box.at[0], box.at[c], sems.at[0, c], sems.at[1, c], back, my_win))

    def swapped(box, sems, side):
        for c in range(1, offs):
            bytes_in(box.at[c], sems.at[side, c])

    to_owner(lambda win: ids_send.at[win], ids_recv, ids_sem.at[0], ids_sem.at[1])

    def kern_of(k):
        return cat([held[k + i] for i in range(GROUP)])

    def pieces_of(box, k, begin):
        c, d = k // wins, lax.rem(k, wins)
        return cat([box[c, d + i, :, begin : begin + slots] for i in range(GROUP)])

    low_iota = lax.broadcasted_iota(jnp.int32, (LOW, width), 0).astype(F32)

    def build_one_hots():
        @pl.loop(0, wins)
        def _(p):
            here = pl.ds(pl.multiple_of(p * slots, slots), slots)
            rays1h_t[here, :] = rays1h[:, here].astype(F32).T.astype(BF16)

        bytes_in(ids_recv.at[0, pl.ds(1, wins - 1)], ids_sem.at[1])
        swap(ids_recv, ids_pair)
        swapped(ids_recv, ids_pair, 1)

        @pl.loop(0, groups)
        def _(g):
            low = pieces_of(ids_recv, g * GROUP, 0)
            high = jnp.broadcast_to(pieces_of(ids_recv, g * GROUP, slots), (16, width))
            hot = jnp.where(low_iota == low, 1.0, 0.0)
            low1h[g] = hot.astype(BF16)
            low1h_t[g] = hot.T.astype(BF16)
            for h in range(HIGH):
                high1h[g, h] = jnp.where(high == h, 1.0, 0.0).astype(BF16)

    def one_step(step, carry):
        data, alpha, rho, rhobar, phibar, sine, cosine = carry
        first = step == 0
        to_owner(lambda win: w_send.at[step, win], w_recv.at[step], w_sem.at[0, step], w_sem.at[1, step])

        @pl.when(first)
        def _():
            each_win(lambda d, to, _: remote(
                kern_hbm.at[to], arrived.at[d], kern_send, kern_recv.at[d // GROUP], my_off, to
            ))
            build_one_hots()

        theta_rho = sine * alpha / rho
        for h in range(HIGH):
            fresh = raw[h] / alpha
            vec[h] = fresh
            srch[h] = fresh - theta_rho * srch[h]
        acc[...] = jnp.zeros_like(acc)

        w_recv[step, 0, 0] = w_send[step, my_win]
        bytes_in(w_recv.at[step, 0, pl.ds(1, wins - 1)], w_sem.at[1, step])
        swap(w_recv.at[step], w_pair.at[step])

        @pl.loop(0, groups)
        def _(g):
            k = g * GROUP

            @pl.when(first & (g < class_groups))
            def _():
                pl.when(g == 0)(lambda: bytes_in(arrived.at[pl.ds(1, GROUP - 1)], kern_recv.at[0]))
                pl.when(g > 0)(lambda: bytes_in(arrived.at[pl.ds(k, GROUP)], kern_recv.at[g]))
                for c in range(1, offs):
                    remote(
                        arrived.at[pl.ds(k, GROUP), half(off_from[c]), :],
                        held.at[pl.ds(c * wins + k, GROUP)],
                        kern_pair.at[0, c], kern_pair.at[1, c * class_groups + g], off_from[c], my_win,
                    )
                for i in range(GROUP):
                    held[k + i] = arrived[k + i, half(my_off), :]

            @pl.when(first & (g >= class_groups))
            def _():
                bytes_in(held.at[pl.ds(k, GROUP)], kern_pair.at[1, g])

            @pl.when(g == class_groups)
            def _():
                swapped(w_recv.at[step], w_pair.at[step], 1)

            row = pieces_of(w_recv.at[step], k, 0)
            parts = split2(kern_of(k) * row)
            rows = []
            for h in range(HIGH):
                mask = jnp.concatenate([high1h[g, h]] * (part // 16), axis=0)
                rows.append(cat([piece * mask for piece in parts]))
            left = jnp.concatenate(rows, axis=0)
            low = low1h_t[g]
            acc[...] += jnp.dot(left, jnp.concatenate([low, low], axis=0), preferred_element_type=F32)

        norms = w_recv[step, :, :, :, slots : 2 * slots].reshape(total, 1, slots)
        beta = jnp.sqrt(total_of(norms))
        data = data / beta
        rho = jnp.sqrt(rhobar * rhobar + beta * beta)
        cosine = rhobar / rho
        sine = beta / rho
        phi = cosine * phibar
        phibar = jnp.where(first, beta, sine * phibar)

        square = jnp.zeros((part, LOW), F32)
        for h in range(HIGH):
            piece = acc[h * part : (h + 1) * part, :] / beta - beta * vec[h]
            raw[h] = piece
            square += piece * piece
            for c, half_piece in enumerate(split2(piece)):
                model[h * part : (h + 1) * part, c * LOW : (c + 1) * LOW] = half_piece
            upd[h] = upd[h] + phi / rho * srch[h]
        norm = fold(jnp.sum(square, axis=0, keepdims=True))

        @pl.loop(0, groups)
        def _(j):
            g = groups - 1 - j
            k = g * GROUP
            low = low1h[g]
            got = jnp.dot(model[...], jnp.concatenate([low, low], axis=0), preferred_element_type=F32)
            high = jnp.broadcast_to(pieces_of(ids_recv, k, slots), (8, width))
            fetched = [jnp.zeros((8, width), F32)] * (part // 8)
            for h in range(HIGH):
                hit = high == h
                for r in range(part // 8):
                    at = h * part + r * 8
                    fetched[r] = jnp.where(hit, got[at : at + 8], fetched[r])
            rows = kern_of(k)
            mixed = sum(fetched[r] * rows[r * 8 : r * 8 + 8] for r in range(part // 8))
            values = jnp.sum(mixed, axis=0, keepdims=True)
            c, d = k // wins, lax.rem(k, wins)
            for i in range(GROUP):
                f_send[step, c, d + i, :, 0:slots] = values[:, i * slots : (i + 1) * slots]
                f_send[step, c, d + i, :, slots : 2 * slots] = norm

            @pl.when(g == class_groups)
            def _():
                each_core(lambda c, to, _: remote(
                    f_send.at[step, c], f_swap.at[step, c], f_pair.at[0, step, c], f_pair.at[1, step, c],
                    to, my_win,
                ))

        for c in range(1, offs):
            bytes_in(f_swap.at[step, c], f_pair.at[1, step, c])
        f_send[step, 0] = f_send[step, 0] + sum(f_swap[step, c] for c in range(1, offs))
        each_win(lambda d, _, back: remote(
            f_send.at[step, 0, d], f_recv.at[step, my_win], f_sem.at[0, step], f_sem.at[1, step], my_off, back
        ))
        f_recv[step, my_win] = f_send[step, 0, 0]
        bytes_in(f_recv.at[step, pl.ds(1, wins - 1)], f_sem.at[1, step])
        alpha = jnp.sqrt(total_of(f_recv[step, :, :, slots : 2 * slots]))
        terms = cat([f_recv[step, p, :, 0:slots] for p in range(wins)])
        data = gather_rays(terms) / alpha - alpha * data
        pl.when(step < ITERS - 1)(lambda: write_weights(step + 1, data))
        rhobar = jnp.where(first, alpha, -cosine * alpha)
        sine = jnp.where(first, jnp.zeros_like(sine), sine)
        return data, alpha, rho, rhobar, phibar, sine, cosine

    one = jnp.ones((1, 1), F32)
    zero = jnp.zeros((1, 1), F32)
    data, alpha, rho, rhobar, phibar, sine, cosine = lax.fori_loop(
        0, ITERS, one_step, (slope_ref[...], one, one, zero, zero, zero, zero)
    )

    s_send[...] = fold(data * data)
    s_recv[0, 0] = s_send[...]
    to_owner(lambda win: s_send, s_recv, w_sem.at[0, ITERS], w_sem.at[1, ITERS])
    theta_rho = sine * alpha / rho
    for h in range(HIGH):
        srch[h] = raw[h] / alpha - theta_rho * srch[h]
    outs = ((upd, out_upd), (srch, out_srch))

    @pl.loop(0, HIGH)
    def _(h):
        for which, (ref, out) in enumerate(outs):
            spot = out.at[half(my_off), pl.ds(pl.multiple_of(h * LOW, LOW), LOW)]
            each_core(lambda c, to, _: remote(
                ref.at[h], spot, pair_send.at[which, c], pair_recv.at[which, c], to, my_win
            ))
            pltpu.make_async_copy(ref.at[h], spot, load_sem.at[which]).start()

    bytes_in(s_recv.at[0, pl.ds(1, wins - 1)], w_sem.at[1, ITERS])
    s_sum[0] = jnp.sum(s_recv[0], axis=0)
    swap(s_sum, s_pair)
    swapped(s_sum, s_pair, 1)
    beta = jnp.sqrt(total_of(s_sum[...]))
    data_ref[...] = data / beta
    rho = jnp.sqrt(rhobar * rhobar + beta * beta)
    phi = rhobar / rho * phibar
    coef_ref[...] = jnp.broadcast_to(phi / rho, coef_ref.shape)
    for which, (_, out) in enumerate(outs):
        bytes_in(out.at[pl.ds(0, part)], load_sem.at[which])
        for c in range(1, offs):
            bytes_in(out.at[pl.ds(0, part)], pair_recv.at[which, c])

    others = pl.ds(1, wins - 1)
    bytes_in(ids_recv.at[0, others], ids_sem.at[0])
    swapped(ids_recv, ids_pair, 0)
    bytes_in(arrived.at[others], kern_send)
    for c in range(1, offs):
        bytes_in(held.at[pl.ds(0, wins)], kern_pair.at[0, c])
    for step in range(ITERS):
        bytes_in(f_recv.at[step, others], f_sem.at[0, step])
        bytes_in(w_recv.at[step, 0, others], w_sem.at[0, step])
        swapped(w_recv.at[step], w_pair.at[step], 0)
        for c in range(1, offs):
            bytes_in(f_swap.at[step, c], f_pair.at[0, step, c])
    bytes_in(s_recv.at[0, others], w_sem.at[0, ITERS])
    swapped(s_sum, s_pair, 0)
    for which, (_, out) in enumerate(outs):
        for c in range(1, offs):
            bytes_in(out.at[pl.ds(0, part)], pair_send.at[which, c])


def body(kernels, blocks, counts, ray_of, slopes):
    offs, wins = lax.axis_size("off"), lax.axis_size("win")
    total = offs * wins
    cells, slots = kernels.shape[3:]
    rays = slopes.shape[2]
    part = cells // offs
    groups = total // GROUP
    ray_low = LOW if rays % LOW == 0 else rays
    vmem = pl.BlockSpec(memory_space=pltpu.VMEM)
    hbm = pl.BlockSpec(memory_space=pltpu.HBM)
    model = (HIGH, part, LOW)
    update, search, coef, data = pl.pallas_call(
        functools.partial(kernel, offs, wins),
        out_shape=(
            jax.ShapeDtypeStruct((cells, BLK_DEV), F32),
            jax.ShapeDtypeStruct((cells, BLK_DEV), F32),
            jax.ShapeDtypeStruct((1, LANES), F32),
            jax.ShapeDtypeStruct((1, rays), F32),
        ),
        in_specs=[hbm] * 5,
        out_specs=(hbm, hbm, vmem, vmem),
        scratch_shapes=[
            pltpu.VMEM((wins, slots), jnp.int32),
            pltpu.SMEM((wins,), jnp.int32),
            pltpu.VMEM((wins, slots), jnp.int32),
            pltpu.VMEM((1, rays), F32),
            pltpu.VMEM((ray_low, wins * slots), BF16),
            pltpu.VMEM((wins * slots, ray_low), BF16),
            pltpu.VMEM((8, wins * slots), jnp.int32),
            pltpu.VMEM((groups, LOW, GROUP * slots), BF16),
            pltpu.VMEM((groups, GROUP * slots, LOW), BF16),
            pltpu.VMEM((groups, HIGH, 16, GROUP * slots), BF16),
            pltpu.VMEM((wins, cells, slots), F32),
            pltpu.VMEM((total, part, slots), F32),
            pltpu.VMEM((wins, 1, 2 * slots), F32),
            pltpu.VMEM((offs, wins, 1, 2 * slots), F32),
            pltpu.VMEM((ITERS, wins, 1, 2 * slots), F32),
            pltpu.VMEM((ITERS, offs, wins, 1, 2 * slots), F32),
            pltpu.VMEM((ITERS, offs, wins, 1, 2 * slots), F32),
            pltpu.VMEM((ITERS, offs, wins, 1, 2 * slots), F32),
            pltpu.VMEM((ITERS, wins, 1, 2 * slots), F32),
            pltpu.VMEM((1, slots), F32),
            pltpu.VMEM((1, wins, 1, slots), F32),
            pltpu.VMEM((offs, 1, slots), F32),
            pltpu.VMEM((HIGH * part, LOW), F32),
            pltpu.VMEM((HIGH * part, 2 * LOW), BF16),
            pltpu.VMEM(model, F32),
            pltpu.VMEM(model, F32),
            pltpu.VMEM(model, F32),
            pltpu.VMEM(model, F32),
            pltpu.SemaphoreType.DMA((2,)),
            pltpu.SemaphoreType.DMA((2, offs)),
            pltpu.SemaphoreType.DMA((2, ITERS + 1)),
            pltpu.SemaphoreType.DMA((ITERS, 2, offs)),
            pltpu.SemaphoreType.DMA((2, ITERS)),
            pltpu.SemaphoreType.DMA((2, ITERS, offs)),
            pltpu.SemaphoreType.DMA((2, offs)),
            pltpu.SemaphoreType.DMA((2, groups)),
            pltpu.SemaphoreType.DMA,
            pltpu.SemaphoreType.DMA((groups,)),
            pltpu.SemaphoreType.DMA((2, offs)),
            pltpu.SemaphoreType.DMA((2, offs)),
            pltpu.SemaphoreType.DMA((5,)),
        ],
        compiler_params=pltpu.CompilerParams(
            collective_id=0, has_side_effects=True, vmem_limit_bytes=60 * 1024 * 1024
        ),
    )(kernels, blocks, counts, ray_of, slopes)
    return update + coef[0, 0] * search, data[None]


def solution(mesh):
    in_specs = (
        P("off", "win", None, None, None),
        P("off", "win", None, None),
        P("off", "win", None),
        P("off", "win", None, None),
        P("off", "win", None),
    )
    out_specs = (P(None, "win"), P("off", "win", None))
    return jax.shard_map(body, mesh=mesh, in_specs=in_specs, out_specs=out_specs, check_vma=False)
```

```python
import functools

import jax
import jax.numpy as jnp
from jax import lax
from jax.experimental import pallas as pl
from jax.experimental.pallas import tpu as pltpu
from jax.sharding import PartitionSpec as P

BLK_DEV = 2048
ITERS = 3
LOW = 256
HIGH = BLK_DEV // LOW
GROUP = 8
LANES = 128

F32 = jnp.float32
BF16 = jnp.bfloat16
MESH = pl.DeviceIdType.MESH


def split2(x):
    top = x.astype(BF16)
    rest = (x - top.astype(F32)).astype(BF16)
    return top, rest


def rows_of(x):
    a = x.astype(BF16).astype(F32)
    b = (x - a).astype(BF16).astype(F32)
    c = x - a - b
    shape = (8, x.shape[1])
    i = lax.broadcasted_iota(jnp.int32, shape, 0)
    wide = lambda y: jnp.broadcast_to(y, shape)
    zero = jnp.zeros(shape, F32)
    return jnp.where(i == 0, wide(a), jnp.where(i == 1, wide(b), jnp.where(i == 2, wide(c), zero)))


def fold(x):
    return sum(x[:, i : i + LANES] for i in range(0, x.shape[1], LANES))


def kernel(
    offs, wins, kern_hbm, block_hbm, count_hbm, ray_hbm, slope_hbm,
    out_ref, data_ref,
    block_ref, count_ref, ray_ref, slope_ref,
    rays1h, rays1h_t, ray_high, low1h, low1h_t, high1h, arrived, held,
    ids_send, ids_recv, w_send, w_recv, f_send, f_swap, f_recv, s_send, s_recv, s_sum,
    acc, model, vec, raw, upd, srch,
    ids_sem, ids_pair, w_sem, w_pair, f_sem, f_pair, s_pair, kern_pair, kern_send, kern_recv, pair_send, pair_recv, load_sem,
):
    kern_hbm, block_hbm, count_hbm, ray_hbm = (x.at[0, 0] for x in (kern_hbm, block_hbm, count_hbm, ray_hbm))
    slope_hbm = slope_hbm.at[0]
    total = offs * wins
    part = kern_hbm.shape[1] // offs
    slots = kern_hbm.shape[2]
    ray_low = rays1h.shape[0]
    ray_parts = slope_ref.shape[1] // ray_low
    groups = total // GROUP
    width = GROUP * slots
    class_groups = wins // GROUP
    my_off = lax.axis_index("off")
    my_win = lax.axis_index("win")
    me = my_win * offs + my_off
    half = lambda o: pl.ds(pl.multiple_of(o * part, 8), part)
    off_to = [lax.rem(my_off + d, offs) for d in range(offs)]
    off_from = [lax.rem(my_off + offs - d, offs) for d in range(offs)]
    win_to = lambda d: lax.rem(my_win + d, wins)
    win_from = lambda d: lax.rem(my_win + wins - d, wins)

    def each_win(act):
        @pl.loop(1, wins)
        def _(d):
            act(d, win_to(d), win_from(d))

    def each_core(act):
        for c in range(1, offs):
            act(c, off_to[c], off_from[c])

    def remote(src, dst, s_sem, r_sem, core, win):
        pltpu.make_async_remote_copy(
            src_ref=src, dst_ref=dst, send_sem=s_sem, recv_sem=r_sem,
            device_id=(core, win), device_id_type=MESH,
        ).start()

    loads = [
        pltpu.make_async_copy(src, dst, load_sem.at[i])
        for i, (src, dst) in enumerate(
            ((count_hbm, count_ref), (ray_hbm, ray_ref), (slope_hbm, slope_ref), (block_hbm, block_ref))
        )
    ]
    loads.append(pltpu.make_async_copy(kern_hbm.at[my_win], arrived.at[0], load_sem.at[4]))
    for load in loads:
        load.start()

    barrier = pltpu.get_barrier_semaphore()
    greet = lambda core, win: pl.semaphore_signal(
        barrier, inc=1, device_id=(core, win), device_id_type=MESH
    )
    each_win(lambda d, to, _: greet(my_off, to))
    each_core(lambda c, to, _: greet(to, my_win))
    for load in loads:
        load.wait()

    ray_iota = lax.broadcasted_iota(jnp.int32, (ray_low, slots), 0)
    lane = lax.broadcasted_iota(jnp.int32, (1, slots), 1)
    for p in range(wins):
        ids = ray_ref[p : p + 1, :]
        high = ids // ray_low
        low = jnp.where(lane < count_ref[p], ids - high * ray_low, -1)
        rays1h[:, p * slots : (p + 1) * slots] = jnp.where(ray_iota == low, 1.0, 0.0).astype(BF16)
        ray_high[:, p * slots : (p + 1) * slots] = jnp.broadcast_to(high, (8, slots))

    def cat(pieces):
        return jnp.concatenate(pieces, axis=1)

    def take(data):
        left = jnp.concatenate(
            [rows_of(data[:, r * ray_low : (r + 1) * ray_low]) for r in range(ray_parts)], axis=0
        ).astype(BF16)
        got = jnp.dot(left, rays1h[...], preferred_element_type=F32)
        high = ray_high[...]
        picked = sum(jnp.where(high == r, got[8 * r : 8 * r + 8], 0.0) for r in range(ray_parts))
        return jnp.sum(picked, axis=0, keepdims=True)

    def gather_rays(values):
        rows = rows_of(values)
        high = ray_high[...]
        left = jnp.concatenate(
            [jnp.where(high == r, rows, 0.0) for r in range(ray_parts)], axis=0
        ).astype(BF16)
        got = jnp.dot(left, rays1h_t[...], preferred_element_type=F32)
        return cat([jnp.sum(got[8 * r : 8 * r + 8], axis=0, keepdims=True) for r in range(ray_parts)])

    def total_of(partials):
        return jnp.sum(jnp.sum(partials, axis=0), axis=1, keepdims=True)

    def bytes_in(ref, sem):
        pltpu.make_async_copy(ref, ref, sem).wait()

    for p in range(wins):
        ids = block_ref[p : p + 1, :]
        high = ids // LOW
        ids_send[p, :, 0:slots] = (ids - high * LOW).astype(F32)
        ids_send[p, :, slots : 2 * slots] = high.astype(F32)
    ids_recv[0, 0] = ids_send[my_win]
    vec[...] = jnp.zeros_like(vec)
    srch[my_off] = jnp.zeros_like(vec)
    upd[my_off] = jnp.zeros_like(vec)
    raw[...] = jnp.zeros_like(raw)

    pl.semaphore_wait(barrier, wins - 1 + offs - 1)

    def to_owner(source_of, box, s_sem, r_sem):
        each_win(lambda d, to, _: remote(source_of(to), box.at[0, d], s_sem, r_sem, my_off, to))

    def swap(box, sems):
        each_core(lambda c, _, back: remote(box.at[0], box.at[c], sems.at[0, c], sems.at[1, c], back, my_win))

    def swapped(box, sems, side):
        for c in range(1, offs):
            bytes_in(box.at[c], sems.at[side, c])

    to_owner(lambda win: ids_send.at[win], ids_recv, ids_sem.at[0], ids_sem.at[1])

    def kern_of(k):
        return cat([held[k + i] for i in range(GROUP)])

    def pieces_of(box, k, begin):
        c, d = k // wins, lax.rem(k, wins)
        return cat([box[c, d + i, :, begin : begin + slots] for i in range(GROUP)])

    low_iota = lax.broadcasted_iota(jnp.int32, (LOW, width), 0).astype(F32)

    def build_one_hots():
        @pl.loop(0, wins)
        def _(p):
            here = pl.ds(pl.multiple_of(p * slots, slots), slots)
            rays1h_t[here, :] = rays1h[:, here].astype(F32).T.astype(BF16)

        bytes_in(ids_recv.at[0, pl.ds(1, wins - 1)], ids_sem.at[1])
        swap(ids_recv, ids_pair)
        swapped(ids_recv, ids_pair, 1)

        @pl.loop(0, groups)
        def _(g):
            low = pieces_of(ids_recv, g * GROUP, 0)
            high = jnp.broadcast_to(pieces_of(ids_recv, g * GROUP, slots), (16, width))
            hot = jnp.where(low_iota == low, 1.0, 0.0)
            low1h[g] = hot.astype(BF16)
            low1h_t[g] = hot.T.astype(BF16)
            for h in range(HIGH):
                high1h[g, h] = jnp.where(high == h, 1.0, 0.0).astype(BF16)

    def one_step(step, carry):
        data, alpha, rho, rhobar, phibar, sine, cosine = carry
        first = step == 0
        weights = take(data)
        partial = fold(data * data)
        for p in range(wins):
            w_send[step, p, :, 0:slots] = weights[:, p * slots : (p + 1) * slots]
            w_send[step, p, :, slots : 2 * slots] = partial
        to_owner(lambda win: w_send.at[step, win], w_recv.at[step], w_sem.at[0, step], w_sem.at[1, step])

        @pl.when(first)
        def _():
            each_win(lambda d, to, _: remote(
                kern_hbm.at[to], arrived.at[d], kern_send, kern_recv.at[d // GROUP], my_off, to
            ))
            build_one_hots()

        theta_rho = sine * alpha / rho
        for h in range(HIGH):
            fresh = raw[h] / alpha
            vec[h] = fresh
            srch[my_off, h] = fresh - theta_rho * srch[my_off, h]
        acc[...] = jnp.zeros_like(acc)

        w_recv[step, 0, 0] = w_send[step, my_win]
        bytes_in(w_recv.at[step, 0, pl.ds(1, wins - 1)], w_sem.at[1, step])
        swap(w_recv.at[step], w_pair.at[step])

        @pl.loop(0, groups)
        def _(g):
            k = g * GROUP

            @pl.when(first & (g < class_groups))
            def _():
                pl.when(g == 0)(lambda: bytes_in(arrived.at[pl.ds(1, GROUP - 1)], kern_recv.at[0]))
                pl.when(g > 0)(lambda: bytes_in(arrived.at[pl.ds(k, GROUP)], kern_recv.at[g]))
                for c in range(1, offs):
                    remote(
                        arrived.at[pl.ds(k, GROUP), half(off_from[c]), :],
                        held.at[pl.ds(c * wins + k, GROUP)],
                        kern_pair.at[0, c], kern_pair.at[1, c * class_groups + g], off_from[c], my_win,
                    )
                for i in range(GROUP):
                    held[k + i] = arrived[k + i, half(my_off), :]

            @pl.when(first & (g >= class_groups))
            def _():
                bytes_in(held.at[pl.ds(k, GROUP)], kern_pair.at[1, g])

            @pl.when(g == class_groups)
            def _():
                swapped(w_recv.at[step], w_pair.at[step], 1)

            row = pieces_of(w_recv.at[step], k, 0)
            parts = split2(kern_of(k) * row)
            rows = []
            for h in range(HIGH):
                mask = jnp.concatenate([high1h[g, h]] * (part // 16), axis=0)
                rows.append(cat([piece * mask for piece in parts]))
            left = jnp.concatenate(rows, axis=0)
            low = low1h_t[g]
            acc[...] += jnp.dot(left, jnp.concatenate([low, low], axis=0), preferred_element_type=F32)

        norms = w_recv[step, :, :, :, slots : 2 * slots].reshape(total, 1, slots)
        beta = jnp.sqrt(total_of(norms))
        data = data / beta
        rho = jnp.sqrt(rhobar * rhobar + beta * beta)
        cosine = rhobar / rho
        sine = beta / rho
        phi = cosine * phibar
        phibar = jnp.where(first, beta, sine * phibar)

        square = jnp.zeros((part, LOW), F32)
        for h in range(HIGH):
            piece = acc[h * part : (h + 1) * part, :] / beta - beta * vec[h]
            raw[h] = piece
            square += piece * piece
            for c, half_piece in enumerate(split2(piece)):
                model[h * part : (h + 1) * part, c * LOW : (c + 1) * LOW] = half_piece
            upd[my_off, h] = upd[my_off, h] + phi / rho * srch[my_off, h]
        norm = fold(jnp.sum(square, axis=0, keepdims=True))

        @pl.loop(0, groups)
        def _(j):
            g = groups - 1 - j
            k = g * GROUP
            low = low1h[g]
            got = jnp.dot(model[...], jnp.concatenate([low, low], axis=0), preferred_element_type=F32)
            high = jnp.broadcast_to(pieces_of(ids_recv, k, slots), (8, width))
            fetched = [jnp.zeros((8, width), F32)] * (part // 8)
            for h in range(HIGH):
                hit = high == h
                for r in range(part // 8):
                    at = h * part + r * 8
                    fetched[r] = jnp.where(hit, got[at : at + 8], fetched[r])
            rows = kern_of(k)
            mixed = sum(fetched[r] * rows[r * 8 : r * 8 + 8] for r in range(part // 8))
            values = jnp.sum(mixed, axis=0, keepdims=True)
            c, d = k // wins, lax.rem(k, wins)
            for i in range(GROUP):
                f_send[step, c, d + i, :, 0:slots] = values[:, i * slots : (i + 1) * slots]
                f_send[step, c, d + i, :, slots : 2 * slots] = norm

            @pl.when(g == class_groups)
            def _():
                each_core(lambda c, to, _: remote(
                    f_send.at[step, c], f_swap.at[step, c], f_pair.at[0, step, c], f_pair.at[1, step, c],
                    to, my_win,
                ))

        for c in range(1, offs):
            bytes_in(f_swap.at[step, c], f_pair.at[1, step, c])
        f_send[step, 0] = f_send[step, 0] + sum(f_swap[step, c] for c in range(1, offs))
        each_win(lambda d, _, back: remote(
            f_send.at[step, 0, d], f_recv.at[step, my_win], f_sem.at[0, step], f_sem.at[1, step], my_off, back
        ))
        f_recv[step, my_win] = f_send[step, 0, 0]
        bytes_in(f_recv.at[step, pl.ds(1, wins - 1)], f_sem.at[1, step])
        alpha = jnp.sqrt(total_of(f_recv[step, :, :, slots : 2 * slots]))
        terms = cat([f_recv[step, p, :, 0:slots] for p in range(wins)])
        data = gather_rays(terms) / alpha - alpha * data
        rhobar = jnp.where(first, alpha, -cosine * alpha)
        sine = jnp.where(first, jnp.zeros_like(sine), sine)
        return data, alpha, rho, rhobar, phibar, sine, cosine

    one = jnp.ones((1, 1), F32)
    zero = jnp.zeros((1, 1), F32)
    data, alpha, rho, rhobar, phibar, sine, cosine = lax.fori_loop(
        0, ITERS, one_step, (slope_ref[...], one, one, zero, zero, zero, zero)
    )

    s_send[...] = fold(data * data)
    s_recv[0, 0] = s_send[...]
    to_owner(lambda win: s_send, s_recv, w_sem.at[0, ITERS], w_sem.at[1, ITERS])
    theta_rho = sine * alpha / rho
    for h in range(HIGH):
        srch[my_off, h] = raw[h] / alpha - theta_rho * srch[my_off, h]
    for other in range(1, offs):
        for which, ref in enumerate((upd, srch)):
            pltpu.make_async_remote_copy(
                src_ref=ref.at[my_off], dst_ref=ref.at[my_off],
                send_sem=pair_send.at[which, other], recv_sem=pair_recv.at[which, other],
                device_id=(off_to[other], my_win), device_id_type=MESH,
            ).start()
    bytes_in(s_recv.at[0, pl.ds(1, wins - 1)], w_sem.at[1, ITERS])
    s_sum[0] = jnp.sum(s_recv[0], axis=0)
    swap(s_sum, s_pair)
    swapped(s_sum, s_pair, 1)
    beta = jnp.sqrt(total_of(s_sum[...]))
    data_ref[...] = data / beta
    rho = jnp.sqrt(rhobar * rhobar + beta * beta)
    phi = rhobar / rho * phibar
    for other in range(1, offs):
        for which, ref in enumerate((upd, srch)):
            bytes_in(ref.at[0], pair_recv.at[which, other])
    for o in range(offs):
        for h in range(HIGH):
            out_ref[o * part : (o + 1) * part, h * LOW : (h + 1) * LOW] = (
                upd[o, h] + phi / rho * srch[o, h]
            )

    others = pl.ds(1, wins - 1)
    bytes_in(ids_recv.at[0, others], ids_sem.at[0])
    swapped(ids_recv, ids_pair, 0)
    bytes_in(arrived.at[others], kern_send)
    for c in range(1, offs):
        bytes_in(held.at[pl.ds(0, wins)], kern_pair.at[0, c])
    for step in range(ITERS):
        bytes_in(f_recv.at[step, others], f_sem.at[0, step])
        bytes_in(w_recv.at[step, 0, others], w_sem.at[0, step])
        swapped(w_recv.at[step], w_pair.at[step], 0)
        for c in range(1, offs):
            bytes_in(f_swap.at[step, c], f_pair.at[0, step, c])
    bytes_in(s_recv.at[0, others], w_sem.at[0, ITERS])
    swapped(s_sum, s_pair, 0)
    for other in range(1, offs):
        for which, ref in enumerate((upd, srch)):
            bytes_in(ref.at[0], pair_send.at[which, other])


def hand_on(update_ref, data_ref, update_out, data_out):
    update_out[...] = update_ref[...]
    data_out[0] = data_ref[...]


def body(kernels, blocks, counts, ray_of, slopes):
    offs, wins = lax.axis_size("off"), lax.axis_size("win")
    total = offs * wins
    cells, slots = kernels.shape[3:]
    rays = slopes.shape[2]
    part = cells // offs
    groups = total // GROUP
    ray_low = LOW if rays % LOW == 0 else rays
    vmem = pl.BlockSpec(memory_space=pltpu.VMEM)
    model = (HIGH, part, LOW)
    update, data = pl.pallas_call(
        functools.partial(kernel, offs, wins),
        out_shape=(
            jax.ShapeDtypeStruct((cells, BLK_DEV), F32),
            jax.ShapeDtypeStruct((1, rays), F32),
        ),
        in_specs=[pl.BlockSpec(memory_space=pltpu.HBM)] * 5,
        out_specs=(vmem, vmem),
        scratch_shapes=[
            pltpu.VMEM((wins, slots), jnp.int32),
            pltpu.SMEM((wins,), jnp.int32),
            pltpu.VMEM((wins, slots), jnp.int32),
            pltpu.VMEM((1, rays), F32),
            pltpu.VMEM((ray_low, wins * slots), BF16),
            pltpu.VMEM((wins * slots, ray_low), BF16),
            pltpu.VMEM((8, wins * slots), jnp.int32),
            pltpu.VMEM((groups, LOW, GROUP * slots), BF16),
            pltpu.VMEM((groups, GROUP * slots, LOW), BF16),
            pltpu.VMEM((groups, HIGH, 16, GROUP * slots), BF16),
            pltpu.VMEM((wins, cells, slots), F32),
            pltpu.VMEM((total, part, slots), F32),
            pltpu.VMEM((wins, 1, 2 * slots), F32),
            pltpu.VMEM((offs, wins, 1, 2 * slots), F32),
            pltpu.VMEM((ITERS, wins, 1, 2 * slots), F32),
            pltpu.VMEM((ITERS, offs, wins, 1, 2 * slots), F32),
            pltpu.VMEM((ITERS, offs, wins, 1, 2 * slots), F32),
            pltpu.VMEM((ITERS, offs, wins, 1, 2 * slots), F32),
            pltpu.VMEM((ITERS, wins, 1, 2 * slots), F32),
            pltpu.VMEM((1, slots), F32),
            pltpu.VMEM((1, wins, 1, slots), F32),
            pltpu.VMEM((offs, 1, slots), F32),
            pltpu.VMEM((HIGH * part, LOW), F32),
            pltpu.VMEM((HIGH * part, 2 * LOW), BF16),
            pltpu.VMEM(model, F32),
            pltpu.VMEM(model, F32),
            pltpu.VMEM((offs,) + model, F32),
            pltpu.VMEM((offs,) + model, F32),
            pltpu.SemaphoreType.DMA((2,)),
            pltpu.SemaphoreType.DMA((2, offs)),
            pltpu.SemaphoreType.DMA((2, ITERS + 1)),
            pltpu.SemaphoreType.DMA((ITERS, 2, offs)),
            pltpu.SemaphoreType.DMA((2, ITERS)),
            pltpu.SemaphoreType.DMA((2, ITERS, offs)),
            pltpu.SemaphoreType.DMA((2, offs)),
            pltpu.SemaphoreType.DMA((2, groups)),
            pltpu.SemaphoreType.DMA,
            pltpu.SemaphoreType.DMA((groups,)),
            pltpu.SemaphoreType.DMA((2, offs)),
            pltpu.SemaphoreType.DMA((2, offs)),
            pltpu.SemaphoreType.DMA((5,)),
        ],
        compiler_params=pltpu.CompilerParams(
            collective_id=0, has_side_effects=True, vmem_limit_bytes=60 * 1024 * 1024
        ),
    )(kernels, blocks, counts, ray_of, slopes)
    return pl.pallas_call(
        hand_on,
        out_shape=(
            jax.ShapeDtypeStruct((cells, BLK_DEV), F32),
            jax.ShapeDtypeStruct((1, 1, rays), F32),
        ),
        in_specs=[vmem, vmem],
        out_specs=(vmem, vmem),
        compiler_params=pltpu.CompilerParams(vmem_limit_bytes=60 * 1024 * 1024),
    )(update, data)


def solution(mesh):
    in_specs = (
        P("off", "win", None, None, None),
        P("off", "win", None, None),
        P("off", "win", None),
        P("off", "win", None, None),
        P("off", "win", None),
    )
    out_specs = (P(None, "win"), P("off", "win", None))
    return jax.shard_map(body, mesh=mesh, in_specs=in_specs, out_specs=out_specs, check_vma=False)
```
